32 devices in a mesh: dp: 4 (over y, core), wide: 8 (over z, x).
Axes of the slice: x: 2, y: 2, z: 4, core: 2. Of those that a mesh axis runs over, the one named last changes fastest.
Arguments:
- tokens: bfloat16 [32768, 768], P(('dp', 'wide')), may hold values from -6 to 6
- lengths: int32 [512], P(('dp', 'wide')), may hold values from 8 to 64
- indices: int32 [512, 10], P(('dp', 'wide')), may hold values from 0 to 8191, as said below
- memory_table: bfloat16 [8192, 3072], P('wide'), may hold values from -6 to 6
- w_query: bfloat16 [768, 768], P('dp'), may hold values from -0.078125 to 0.078125
- w_key: bfloat16 [768, 768], P('dp'), may hold values from -0.21875 to 0.21875
- w_value: bfloat16 [768, 768], P('dp'), may hold values from -0.21875 to 0.21875
- w_out: bfloat16 [768, 768], P('dp'), may hold values from -0.625 to 0.625
- w_in: bfloat16 [768, 3072], P('dp'), may hold values from -0.21875 to 0.21875
- w_back: bfloat16 [3072, 768], P('dp'), may hold values from -0.109375 to 0.109375
- gain_one: bfloat16 [768], P('dp'), may hold values from 0.5 to 1.5
- gain_two: bfloat16 [768], P('dp'), may hold values from 0.5 to 1.5
- rel_bias: bfloat16 [32, 12], P('dp'), may hold values from -4 to 4
- cotangent: bfloat16 [32768, 768], P(('dp', 'wide')), may hold values from -6 to 6
Outputs:
- layer_out: bfloat16 [32768, 768], P(('dp', 'wide'))
- grad_tokens: float32 [32768, 768], P(('dp', 'wide'))
- grad_query: float32 [768, 768], P('dp')
- grad_key: float32 [768, 768], P('dp')
- grad_value: float32 [768, 768], P('dp')
- grad_out: float32 [768, 768], P('dp')
- grad_in: float32 [768, 3072], P('dp')
- grad_back: float32 [3072, 768], P('dp')
- grad_gain_one: float32 [768], P('dp')
- grad_gain_two: float32 [768], P('dp')
- grad_bias: float32 [32, 12], P('dp')
- grad_table: float32 [8192, 3072], P('wide', 'dp')
The draws below stay inside these ranges and needn't reach their ends.
Inputs may be any that keep to these rules, and one draw needn't show every extreme that they name: `indices`: row n of memory_table is held by index n // 1024 of wide. The 16 questions of one device name at most 21 rows held by any one index of wide, and exactly 21 held by some index; the first, the middle and the last index are named by every device's questions. Rows may repeat.
All inputs are finite; a program needn't handle non-finite values.
Results may differ from the reference program's by a relative error of at most 0.02.
Values may be sent and summed in bfloat16 or wider, within the bound.
No kernel may reach another device: no remote copies, remote signals or barrier semaphores. Data moves between devices by JAX's collectives and lax.ppermute only.
A program may use at most 192 MiB of HBM per device.

```python
import math
import jax
import jax.numpy as jnp
import numpy as np
from jax import lax

D = 768
HEADS = 12
HD = 64
FF = 3072
NB = 32
MAXDIST = 128
QLEN = 64
TOPK = 10
QDEV = 16
ENT_DEV = 1024
QUESTIONS = 512
TOKENS = 32768
ENTRIES = 8192
CAP = 21


def draw_indices(key, part):
    key = jax.random.fold_in(key, 7)
    owner_total = ENTRIES // ENT_DEV
    block_total = QUESTIONS // QDEV
    per_block = QDEV * TOPK
    pool_size = owner_total * CAP
    pool_owner = jnp.repeat(jnp.arange(owner_total, dtype=jnp.int32), CAP)
    pool_copy = jnp.tile(jnp.arange(CAP, dtype=jnp.int32), owner_total)
    middle = owner_total // 2

    def one_block(block_key):
        key_top, key_rank, key_order, key_entry = jax.random.split(block_key, 4)
        top_owner = jax.random.randint(key_top, (), 1, owner_total - 2)
        top_owner = jnp.where(top_owner >= middle, top_owner + 1, top_owner)
        special = (pool_copy == 0) & ((pool_owner == 0) | (pool_owner == middle) | (pool_owner == owner_total - 1))
        favored = (pool_owner == top_owner) | special
        ranking = jax.random.permutation(key_rank, pool_size).astype(jnp.int32) - favored.astype(jnp.int32) * pool_size
        ordering = jnp.argsort(ranking)
        chosen = pool_owner[ordering[:per_block]]
        chosen = jax.random.permutation(key_order, chosen)
        entry_ids = jax.random.randint(key_entry, (per_block,), 0, ENT_DEV)
        return (chosen * ENT_DEV + entry_ids).astype(jnp.int32).reshape(QDEV, TOPK)
    return jax.vmap(one_block)(jax.random.split(key, block_total)).reshape(QUESTIONS, TOPK)


def place_ends(entries, rng, least, high):
    shape = entries.shape
    spot = [jax.random.randint(jax.random.fold_in(rng, axis), (), 0, shape[axis]) for axis in range(len(shape))]
    entries = entries.at[tuple(spot)].set(least)
    longest = shape.index(max(shape))
    spot[longest] = (spot[longest] + 1) % shape[longest]
    return entries.at[tuple(spot)].set(high)


def block_scale(rng, dims, shards, least, largest):
    gain = 1.0
    for position, parts in shards:
        draws = jax.random.uniform(jax.random.fold_in(jax.random.fold_in(rng, 6), position), (parts,), jnp.float32, least / len(shards), largest / len(shards))
        gain = gain * jnp.repeat(jnp.exp(draws), dims[position] // parts).reshape((-1,) + (1,) * (len(dims) - 1 - position))
    return gain


def bell_draw(stream_key, extent, deviation, most, cuts=(), kind=jnp.bfloat16):
    entries = jax.random.normal(stream_key, extent, jnp.float32) * deviation
    if len(cuts) > 0:
        entries = block_scale(stream_key, extent, cuts, -0.22, 0.18) * entries
    return jnp.clip(entries, min=-most, max=most).astype(kind)


def setup_inputs(seed: int = 0) -> dict:
    key_of = jax.random.split(jax.random.key(seed), 15)
    tokens = bell_draw(key_of[0], (TOKENS, D), 1.0, 6.0, ((0, 32),))
    lengths = place_ends(jax.random.randint(key_of[1], (QUESTIONS,), QLEN // 8, QLEN + 1), jax.random.fold_in(key_of[1], 1), QLEN // 8, QLEN).astype(jnp.int32)
    indices = draw_indices(jax.random.fold_in(key_of[14], 71), 0)
    memory_table = bell_draw(key_of[3], (ENTRIES, 4 * D), 1.0, 6.0, ((0, 8),))
    w_query = bell_draw(key_of[4], (D, D), (8 * D) ** -0.5, 0.078125, ((0, 4),))
    w_key = bell_draw(key_of[5], (D, D), D ** -0.5, 0.21875, ((0, 4),))
    w_value = bell_draw(key_of[6], (D, D), D ** -0.5, 0.21875, ((0, 4),))
    w_out = bell_draw(key_of[7], (D, D), (D // 8) ** -0.5, 0.625, ((0, 4),))
    w_in = bell_draw(key_of[8], (D, FF), D ** -0.5, 0.21875, ((0, 4),))
    w_back = bell_draw(key_of[9], (FF, D), FF ** -0.5, 0.109375, ((0, 4),))
    gain_one = jnp.clip(1.0 + 0.1 * jax.random.normal(key_of[10], (D,), jnp.float32), 0.5, 1.5).astype(jnp.bfloat16)
    gain_two = jnp.clip(1.0 + 0.1 * jax.random.normal(key_of[11], (D,), jnp.float32), 0.5, 1.5).astype(jnp.bfloat16)
    rel_bias = bell_draw(key_of[12], (NB, HEADS), 1.0, 4.0, ((0, 4),))
    cotangent = bell_draw(key_of[13], (TOKENS, D), 1.0, 6.0, ((0, 32),))
    return dict(tokens=tokens, lengths=lengths, indices=indices, memory_table=memory_table, w_query=w_query, w_key=w_key, w_value=w_value, w_out=w_out, w_in=w_in, w_back=w_back, gain_one=gain_one, gain_two=gain_two, rel_bias=rel_bias, cotangent=cotangent)


@jax.custom_vjp
def low(v):
    return lax.optimization_barrier(v.astype(jnp.bfloat16)).astype(jnp.float32)

@jax.custom_vjp
def low_back(v):
    return v

def low_keep(v):
    return (low(v), None)

def low_pass(kept, grad):
    return (grad,)

def back_keep(v):
    return (v, None)

def back_low(kept, grad):
    return (low(grad),)
low.defvjp(low_keep, low_pass)
low_back.defvjp(back_keep, back_low)
exact_mode = lax.Precision.HIGHEST

def bucket_table(length, buckets, max_reach):
    half_count = buckets // 2
    near_count = half_count // 2
    onehot = np.zeros((length * length, buckets), np.float32)
    for target in range(length):
        for source in range(length):
            offset = source - target
            bucket = half_count if offset > 0 else 0
            distance = abs(offset)
            if distance < near_count:
                bucket += distance
            else:
                bucket += min(half_count - 1, near_count + int(math.log(distance / near_count) / math.log(max_reach / near_count) * (half_count - near_count)))
            onehot[target * length + source, bucket] = 1.0
    return onehot

def rms_scale(values, gain_vec):
    return values * lax.rsqrt(lax.optimization_barrier(jnp.mean(values * values, axis=-1, keepdims=True)) + 1e-06) * gain_vec

def matmul(left_side, right_side):
    return jnp.dot(left_side, right_side, precision=exact_mode)

def layer_block(weights, table_rows, tokens_block, lengths_block, indices_block):
    w_query, w_key, w_value, w_out, w_in, w_back, gain_one, gain_two, rel_bias = weights
    question_count = lengths_block.shape[0]
    model_width = tokens_block.shape[1]
    normed = low(rms_scale(tokens_block, gain_one))
    queries = low(low_back(matmul(normed, w_query)))
    keys = low(low_back(matmul(normed, w_key)))
    values = low(low_back(matmul(normed, w_value)))
    prefix = jnp.take(table_rows, indices_block.reshape(-1), axis=0).reshape(question_count, TOPK, 4, model_width)
    prefix_keys = prefix[:, :, 0:2].reshape(question_count, 2 * TOPK, HEADS, HD)
    prefix_values = prefix[:, :, 2:4].reshape(question_count, 2 * TOPK, HEADS, HD)
    all_keys = jnp.concatenate([prefix_keys, keys.reshape(question_count, QLEN, HEADS, HD)], axis=1)
    all_values = jnp.concatenate([prefix_values, values.reshape(question_count, QLEN, HEADS, HD)], axis=1)
    query_heads = queries.reshape(question_count, QLEN, HEADS, HD)
    onehot = jnp.asarray(bucket_table(QLEN, NB, MAXDIST), jnp.float32)
    position_bias = matmul(onehot, rel_bias).reshape(QLEN, QLEN, HEADS).transpose(2, 0, 1)
    bias_full = jnp.concatenate([jnp.zeros((HEADS, QLEN, 2 * TOPK), jnp.float32), position_bias], axis=2)
    scores = jnp.einsum('bihd,bjhd->bhij', query_heads, all_keys, precision=exact_mode)
    scores = low_back(scores + bias_full[None])
    token_valid = jnp.arange(QLEN)[None, :] < lengths_block[:, None]
    key_valid = jnp.concatenate([jnp.ones((question_count, 2 * TOPK), bool), token_valid], axis=1)
    masked = jnp.where(key_valid[:, None, None, :], scores, -1000000000.0)
    probs_low = low(jax.nn.softmax(masked, axis=-1))
    context = jnp.einsum('bhij,bjhd->bihd', probs_low, all_values, precision=exact_mode)
    context = low(low_back(context.reshape(question_count * QLEN, model_width)))
    middle = tokens_block + low_back(matmul(context, w_out))
    normed_two = low(rms_scale(middle, gain_two))
    hidden = low_back(matmul(normed_two, w_in))
    active = low(jax.nn.gelu(hidden, approximate=True))
    return middle + low_back(matmul(active, w_back))

def forward(weights, table_rows, tokens_all, lengths, indices):
    block_total = QUESTIONS // QDEV
    pieces_all = (tokens_all.reshape(block_total, QDEV * QLEN, D), lengths.reshape(block_total, QDEV), indices.reshape(block_total, QDEV, TOPK))
    block_step = jax.checkpoint(lambda weight_set, table_set, pieces: layer_block(weight_set, table_set, pieces[0], pieces[1], pieces[2]))

    def scan_step(carry, pieces):
        return (carry, block_step(weights, table_rows, pieces))
    _, outputs = lax.scan(scan_step, jnp.zeros((), jnp.float32), pieces_all)
    return outputs.reshape(TOKENS, D)

def reference(tokens, lengths, indices, memory_table, w_query, w_key, w_value, w_out, w_in, w_back, gain_one, gain_two, rel_bias, cotangent):
    weights = tuple((item.astype(jnp.float32) for item in (w_query, w_key, w_value, w_out, w_in, w_back, gain_one, gain_two, rel_bias)))
    table_rows = memory_table.astype(jnp.float32)
    inputs = tokens.astype(jnp.float32)
    result, back_fn = jax.vjp(lambda weight_set, table_set, input_set: forward(weight_set, table_set, input_set, lengths, indices), weights, table_rows, inputs)
    weight_grads, table_grad, input_grad = back_fn(cotangent.astype(jnp.float32))
    return (result.astype(jnp.bfloat16), input_grad, weight_grads[0], weight_grads[1], weight_grads[2], weight_grads[3], weight_grads[4], weight_grads[5], weight_grads[6], weight_grads[7], weight_grads[8], table_grad)
```

```python
import math

import jax
import jax.numpy as jnp
import numpy as np
from jax import lax
from jax.experimental import pallas as pl
from jax.experimental.pallas import tpu as pltpu
from jax.sharding import PartitionSpec as P

HEADS = 12
HD = 64
NB = 32
MAXDIST = 128
QLEN = 64
TOPK = 10
PADK = 16
LANES = 128
QUAD = 256
EPS = 1e-06
F32 = jnp.float32
BF16 = jnp.bfloat16
VMEM_BYTES = 58 * 1024 * 1024
ANY = pl.BlockSpec(memory_space=pl.ANY)
SMEM = pl.BlockSpec(memory_space=pltpu.SMEM)


def bucket_table(length, buckets, max_reach):
    half_count = buckets // 2
    near_count = half_count // 2
    onehot = np.zeros((length, length, buckets), np.float32)
    for target in range(length):
        for source in range(length):
            offset = source - target
            bucket = half_count if offset > 0 else 0
            distance = abs(offset)
            if distance < near_count:
                bucket += distance
            else:
                bucket += min(
                    half_count - 1,
                    near_count
                    + int(
                        math.log(distance / near_count)
                        / math.log(max_reach / near_count)
                        * (half_count - near_count)
                    ),
                )
            onehot[target, source, bucket] = 1.0
    return onehot


def mm(a, b):
    return jnp.dot(a, b, preferred_element_type=F32)


def mm_nt(a, b):
    return lax.dot_general(a, b, (((1,), (1,)), ((), ())), preferred_element_type=F32)


def mm_tn(a, b):
    return lax.dot_general(a, b, (((0,), (0,)), ((), ())), preferred_element_type=F32)


def cost(flops, size):
    return pl.CostEstimate(flops=int(flops), bytes_accessed=int(size), transcendentals=0)


def params(grid=True):
    return pltpu.CompilerParams(
        vmem_limit_bytes=VMEM_BYTES,
        **(dict(dimension_semantics=("arbitrary",)) if grid else {}),
    )


def rms_factor(values):
    return lax.rsqrt(jnp.mean(values * values, axis=-1, keepdims=True) + EPS)


def block_copies(member, blocks, first, rows, target, sems):
    return [
        pltpu.make_async_copy(
            block.at[pl.ds(first, rows)],
            target.at[pl.ds(pl.multiple_of((member ^ k) * rows, rows), rows)],
            sems.at[k],
        )
        for k, block in enumerate(blocks)
    ]


def qkv_kernel(nd, rows, me, x_ref, gain_ref, *rest):
    blocks, (q_ref, k_ref, v_ref, n_ref, w, sems) = rest[:nd], rest[nd:]

    @pl.when(pl.program_id(0) == 0)
    def _():
        copies = []
        for i in range(3):
            copies += block_copies(me[0], blocks, i * rows, rows, w.at[i], sems.at[i])
        for c in copies:
            c.start()
        for c in copies:
            c.wait()

    x = x_ref[...].astype(F32)
    normed = (x * rms_factor(x) * gain_ref[...]).astype(BF16)
    n_ref[...] = normed
    for i, out in enumerate((q_ref, k_ref, v_ref)):
        out[...] = mm(normed, w[i]).astype(BF16)


def qkv_call(me, x, gain, blocks, rows, tile):
    nd, (count, width) = len(blocks), x.shape
    row_spec = pl.BlockSpec((tile, width), lambda i: (i, 0))
    return pl.pallas_call(
        lambda *refs: qkv_kernel(nd, rows, *refs),
        grid=(count // tile,),
        in_specs=[SMEM, row_spec, pl.BlockSpec((1, width), lambda i: (0, 0))] + [ANY] * nd,
        out_specs=[row_spec] * 4,
        out_shape=[jax.ShapeDtypeStruct((count, width), BF16)] * 4,
        scratch_shapes=[
            pltpu.VMEM((3, width, width), BF16),
            pltpu.SemaphoreType.DMA((3, nd)),
        ],
        compiler_params=params(),
        cost_estimate=cost(6 * count * width * width, 10 * count * width + 6 * width * width),
        name="norm_qkv",
    )(me, x, gain, *blocks)


def key_list(tok, pre, first):
    width = tok.shape[1]
    return jnp.concatenate(
        [
            tok,
            pre[:, first * width : (first + 1) * width],
            pre[:, (first + 1) * width : (first + 2) * width],
            jnp.zeros((LANES - QLEN - 2 * PADK, width), tok.dtype),
        ],
        axis=0,
    )


def spread_heads(part):
    head = lax.broadcasted_iota(jnp.int32, part.shape, 1) // HD
    return jnp.concatenate(
        [jnp.where(head == h, part, jnp.zeros_like(part)) for h in range(QUAD // HD)], axis=0
    )


def gather_heads(full):
    head = lax.broadcasted_iota(jnp.int32, (QLEN, QUAD), 1) // HD
    out = full[:QLEN]
    for h in range(1, QUAD // HD):
        out = jnp.where(head == h, full[h * QLEN : (h + 1) * QLEN], out)
    return out


def attn_kernel(nd, rows, batch, me, lens, *rest):
    (q_ref, k_ref, v_ref, pre_ref, x_ref, bias_ref, gain_ref) = rest[:7]
    blocks = rest[7 : 7 + nd]
    (p_ref, ctx_ref, mid_ref, n2_ref, w, sems) = rest[7 + nd :]
    step = pl.program_id(0)

    @pl.when(step == 0)
    def _():
        copies = block_copies(me[0], blocks, 3 * rows, rows, w, sems)
        for c in copies:
            c.start()
        for c in copies:
            c.wait()

    lane = lax.broadcasted_iota(jnp.int32, (1, LANES), 1)
    fixed = ((lane >= QLEN) & (lane < QLEN + TOPK)) | (
        (lane >= QLEN + PADK) & (lane < QLEN + PADK + TOPK)
    )
    width = q_ref.shape[1]
    for b in range(batch):
        r = slice(b * QLEN, (b + 1) * QLEN)
        pre = pre_ref[b * PADK : (b + 1) * PADK, :]
        keys = key_list(k_ref[r, :], pre, 0)
        values = key_list(v_ref[r, :], pre, 2)
        valid = fixed | (lane < jnp.minimum(lens[step * batch + b], QLEN))
        for t in range(width // QUAD):
            c = slice(t * QUAD, (t + 1) * QUAD)
            scores = mm_nt(spread_heads(q_ref[r, c]), keys[:, c]) + bias_ref[c, :]
            scores = jnp.where(valid, scores, -1e9)
            e = jnp.exp(scores - jnp.max(scores, axis=1, keepdims=True))
            probs = (e * (1.0 / jnp.sum(e, axis=1, keepdims=True))).astype(BF16)
            p_ref[b, c, :] = probs
            ctx_ref[r, c] = gather_heads(mm(probs, values[:, c])).astype(BF16)
    middle = x_ref[...].astype(F32) + mm(ctx_ref[...], w[...])
    mid_ref[...] = middle
    n2_ref[...] = (middle * rms_factor(middle) * gain_ref[...]).astype(BF16)


def attn_call(me, lens, q, k, v, prefix, x, bias, gain, blocks, rows, batch):
    nd, (count, width) = len(blocks), q.shape
    tile = batch * QLEN
    row_spec = pl.BlockSpec((tile, width), lambda i: (i, 0))
    whole = lambda shape: pl.BlockSpec(shape, lambda i: (0,) * len(shape))
    quest = count // QLEN
    return pl.pallas_call(
        lambda *refs: attn_kernel(nd, rows, batch, *refs),
        grid=(count // tile,),
        in_specs=[SMEM, SMEM, row_spec, row_spec, row_spec]
        + [
            pl.BlockSpec((batch * PADK, prefix.shape[1]), lambda i: (i, 0)),
            row_spec,
            whole(bias.shape),
            whole((1, width)),
        ]
        + [ANY] * nd,
        out_specs=[
            pl.BlockSpec((batch, HEADS * QLEN, LANES), lambda i: (i, 0, 0)),
            row_spec,
            row_spec,
            row_spec,
        ],
        out_shape=[
            jax.ShapeDtypeStruct((quest, HEADS * QLEN, LANES), BF16),
            jax.ShapeDtypeStruct((count, width), BF16),
            jax.ShapeDtypeStruct((count, width), F32),
            jax.ShapeDtypeStruct((count, width), BF16),
        ],
        scratch_shapes=[pltpu.VMEM((width, width), BF16), pltpu.SemaphoreType.DMA((nd,))],
        compiler_params=params(),
        cost_estimate=cost(12 * count * width * width, 20 * count * width),
        name="attention",
    )(me, lens, q, k, v, prefix, x, bias, gain, *blocks)


def ff_kernel(nd, rows, tile, me, n2_ref, mid_ref, g_ref, *rest):
    in_blocks, back_blocks = rest[:nd], rest[nd : 2 * nd]
    (out_ref, dn2_ref, bt_ref, bm_ref, it_ref, im_ref) = rest[2 * nd : 2 * nd + 6]
    (win, wback, act, gh, gin, total, in_sems, back_sems) = rest[2 * nd + 6 :]
    step = pl.program_id(0)
    half = nd // 2
    member = me[0]
    count, width = n2_ref.shape
    chunk = wback.shape[1]
    order = [2 * s + 1 for s in range(half)] + [2 * s for s in range(half)]
    rel = jnp.where(step < half, 2 * step + 1, 2 * (step - half))

    @pl.when(step == 0)
    def _():
        copies = block_copies(member, in_blocks, 0, rows, win, in_sems)
        for c in copies:
            c.start()
        for s, k in enumerate(order):
            c = pltpu.make_async_copy(back_blocks[k], wback.at[s], back_sems.at[s])
            c.start()
            copies.append(c)
        for c in copies:
            c.wait()

    cols = pl.ds(pl.multiple_of((member ^ rel) * chunk, LANES), chunk)
    w_in = win[:, cols]
    w_back = wback[step]

    def row_tile(m, carry):
        r = pl.ds(pl.multiple_of(m * tile, tile), tile)
        h = mm(n2_ref[r, :], w_in)
        h2 = h * h
        th = jnp.tanh(math.sqrt(2 / math.pi) * h * (1.0 + 0.044715 * h2))
        a = (0.5 * h * (1.0 + th)).astype(BF16)
        slope = 0.5 * (1.0 + th) + 0.5 * h * (1.0 - th * th) * (
            math.sqrt(2 / math.pi) * (1.0 + 3 * 0.044715 * h2)
        )
        act[r, :] = a
        y = mm(a, w_back)
        d = (mm_nt(g_ref[r, :], w_back) * slope).astype(BF16)
        gh[r, :] = d
        dn = mm_nt(d, w_in)

        @pl.when(step == 0)
        def _():
            total[r, :] = mid_ref[r, :] + y
            dn2_ref[r, :] = dn

        @pl.when(step > 0)
        def _():
            total[r, :] += y
            dn2_ref[r, :] += dn

        return carry

    lax.fori_loop(0, count // tile, row_tile, 0)

    @pl.when(step < half)
    def _():
        bt_ref[...] = mm_tn(act[...], g_ref[...]).astype(BF16)[None]

    @pl.when(step >= half)
    def _():
        bm_ref[...] = mm_tn(act[...], g_ref[...]).astype(BF16)[None]

    gin[:, cols] = mm_tn(n2_ref[...], gh[...]).astype(BF16)

    @pl.when(step == nd - 1)
    def _():
        out_ref[...] = total[...].astype(BF16)
        for kk in range(half):
            for ref, k in ((it_ref, 2 * kk + 1), (im_ref, 2 * kk)):
                ref[kk] = gin[pl.ds(pl.multiple_of((member ^ k) * rows, rows), rows), :]


def ff_call(me, n2, mid, g, in_blocks, back_blocks, tile):
    nd, (count, width) = len(in_blocks), n2.shape
    half = nd // 2
    rows, hidden = in_blocks[0].shape
    chunk = back_blocks[0].shape[0]
    whole = lambda *shape: pl.BlockSpec(shape, lambda i: (0,) * len(shape))
    return pl.pallas_call(
        lambda *refs: ff_kernel(nd, rows, tile, *refs),
        grid=(nd,),
        in_specs=[SMEM] + [whole(count, width)] * 3 + [ANY] * (2 * nd),
        out_specs=[
            whole(count, width),
            whole(count, width),
            pl.BlockSpec((1, chunk, width), lambda i: (jnp.minimum(i, half - 1), 0, 0)),
            pl.BlockSpec((1, chunk, width), lambda i: (jnp.maximum(i - half, 0), 0, 0)),
            whole(half, rows, hidden),
            whole(half, rows, hidden),
        ],
        out_shape=[
            jax.ShapeDtypeStruct((count, width), BF16),
            jax.ShapeDtypeStruct((count, width), F32),
            jax.ShapeDtypeStruct((half, chunk, width), BF16),
            jax.ShapeDtypeStruct((half, chunk, width), BF16),
            jax.ShapeDtypeStruct((half, rows, hidden), BF16),
            jax.ShapeDtypeStruct((half, rows, hidden), BF16),
        ],
        scratch_shapes=[
            pltpu.VMEM((width, hidden), BF16),
            pltpu.VMEM((nd, chunk, width), BF16),
            pltpu.VMEM((count, chunk), BF16),
            pltpu.VMEM((count, chunk), BF16),
            pltpu.VMEM((width, hidden), BF16),
            pltpu.VMEM((count, width), F32),
            pltpu.SemaphoreType.DMA((nd,)),
            pltpu.SemaphoreType.DMA((nd,)),
        ],
        compiler_params=params(),
        cost_estimate=cost(12 * count * width * hidden, 16 * count * width + 8 * width * hidden),
        name="feed_forward",
    )(me, n2, mid, g, *in_blocks, *back_blocks)


def attn_back_kernel(nd, rows, batch, me, *rest):
    (g_ref, dn2_ref, mid_ref, gain_ref, p_ref, q_ref, k_ref, v_ref, pre_ref) = rest[:9]
    blocks = rest[9 : 9 + nd]
    (gm_ref, gml_ref, dq_ref, dk_ref, dv_ref, dpre_ref, dbias_ref, dgain_ref) = rest[9 + nd : 17 + nd]
    w, sems = rest[17 + nd :]
    step = pl.program_id(0)

    @pl.when(step == 0)
    def _():
        copies = block_copies(me[0], blocks, 3 * rows, rows, w, sems)
        for c in copies:
            c.start()
        dbias_ref[...] = jnp.zeros_like(dbias_ref)
        dgain_ref[...] = jnp.zeros_like(dgain_ref)
        for c in copies:
            c.wait()

    mid, dn2 = mid_ref[...], dn2_ref[...]
    r2 = rms_factor(mid)
    scaled = dn2 * gain_ref[...]
    dgain_ref[...] += jnp.sum(dn2 * mid * r2, axis=0, keepdims=True)
    gm = (
        g_ref[...].astype(F32)
        + r2 * scaled
        - mid * (r2 * r2 * r2 * jnp.mean(scaled * mid, axis=-1, keepdims=True))
    )
    gm_ref[...] = gm
    low = gm.astype(BF16)
    gml_ref[...] = low
    dctx = mm_nt(low, w[...]).astype(BF16)
    width = q_ref.shape[1]
    for b in range(batch):
        r = slice(b * QLEN, (b + 1) * QLEN)
        pr = slice(b * PADK, (b + 1) * PADK)
        pre = pre_ref[pr, :]
        keys = key_list(k_ref[r, :], pre, 0)
        values = key_list(v_ref[r, :], pre, 2)
        for t in range(width // QUAD):
            c = slice(t * QUAD, (t + 1) * QUAD)
            gs = spread_heads(dctx[r, c])
            qs = spread_heads(q_ref[r, c])
            low_probs = p_ref[b, c, :]
            probs = low_probs.astype(F32)
            gp = mm_nt(gs, values[:, c])
            dval = mm_tn(low_probs, gs)
            ds = (probs * (gp - jnp.sum(probs * gp, axis=1, keepdims=True))).astype(BF16)
            dbias_ref[c, :] += ds.astype(F32)
            dq_ref[r, c] = gather_heads(mm(ds, keys[:, c])).astype(BF16)
            dkey = mm_tn(ds, qs)
            for ref, first, grad in ((dk_ref, 0, dkey), (dv_ref, 2, dval)):
                low_grad = grad.astype(BF16)
                ref[r, c] = low_grad[:QLEN]
                for s in range(2):
                    at = (first + s) * width + t * QUAD
                    dpre_ref[pr, at : at + QUAD] = low_grad[
                        QLEN + s * PADK : QLEN + (s + 1) * PADK
                    ]


def attn_back_call(me, g, dn2, mid, gain, probs, q, k, v, prefix, blocks, rows, batch):
    nd, (count, width) = len(blocks), q.shape
    tile = batch * QLEN
    row_spec = pl.BlockSpec((tile, width), lambda i: (i, 0))
    pre_spec = pl.BlockSpec((batch * PADK, prefix.shape[1]), lambda i: (i, 0))
    whole = lambda *shape: pl.BlockSpec(shape, lambda i: (0,) * len(shape))
    rows_of = lambda dtype: jax.ShapeDtypeStruct((count, width), dtype)
    return pl.pallas_call(
        lambda *refs: attn_back_kernel(nd, rows, batch, *refs),
        grid=(count // tile,),
        in_specs=[SMEM, row_spec, row_spec, row_spec, whole(1, width)]
        + [pl.BlockSpec((batch, HEADS * QLEN, LANES), lambda i: (i, 0, 0))]
        + [row_spec] * 3
        + [pre_spec]
        + [ANY] * nd,
        out_specs=[row_spec] * 5 + [pre_spec, whole(HEADS * QLEN, LANES), whole(1, width)],
        out_shape=[rows_of(F32)]
        + [rows_of(BF16)] * 4
        + [
            jax.ShapeDtypeStruct(prefix.shape, BF16),
            jax.ShapeDtypeStruct((HEADS * QLEN, LANES), F32),
            jax.ShapeDtypeStruct((1, width), F32),
        ],
        scratch_shapes=[pltpu.VMEM((width, width), BF16), pltpu.SemaphoreType.DMA((nd,))],
        compiler_params=params(),
        cost_estimate=cost(20 * count * width * width, 30 * count * width),
        name="attention_back",
    )(me, g, dn2, mid, gain, probs, q, k, v, prefix, *blocks)


def square_kernel(nd, rows, me, n_ref, ctx_ref, dq_ref, dk_ref, dv_ref, gml_ref, their, mine, full):
    width = n_ref.shape[1]
    for i, (left, right) in enumerate(
        ((n_ref, dq_ref), (n_ref, dk_ref), (n_ref, dv_ref), (ctx_ref, gml_ref))
    ):
        for c in range(0, width, QUAD):
            full[i, c : c + QUAD, :] = mm_tn(left[:, c : c + QUAD], right[...]).astype(BF16)
        for kk in range(nd // 2):
            for ref, k in ((their, 2 * kk + 1), (mine, 2 * kk)):
                at = pl.ds(pl.multiple_of((me[0] ^ k) * rows, rows), rows)
                ref[kk, i * rows : (i + 1) * rows, :] = full[i, at, :]


def square_call(me, nd, rows, normed, ctx, dq, dk, dv, gml):
    count, width = normed.shape
    vmem = pl.BlockSpec(memory_space=pltpu.VMEM)
    shape = jax.ShapeDtypeStruct((nd // 2, 4 * rows, width), BF16)
    return pl.pallas_call(
        lambda *refs: square_kernel(nd, rows, *refs),
        in_specs=[SMEM] + [vmem] * 6,
        out_specs=[vmem] * 2,
        out_shape=[shape] * 2,
        scratch_shapes=[pltpu.VMEM((4, width, width), BF16)],
        compiler_params=params(False),
        cost_estimate=cost(8 * count * width * width, 12 * count * width + 8 * width * width),
        name="square_grads",
    )(me, normed, ctx, dq, dk, dv, gml)


def input_kernel(nd, rows, me, x_ref, gain_ref, gm_ref, dq_ref, dk_ref, dv_ref, *rest):
    blocks, (gt_ref, dgain_ref, w, sems) = rest[:nd], rest[nd:]

    @pl.when(pl.program_id(0) == 0)
    def _():
        copies = []
        for i in range(3):
            copies += block_copies(me[0], blocks, i * rows, rows, w.at[i], sems.at[i])
        for c in copies:
            c.start()
        dgain_ref[...] = jnp.zeros_like(dgain_ref)
        for c in copies:
            c.wait()

    dn = mm_nt(dq_ref[...], w[0]) + mm_nt(dk_ref[...], w[1]) + mm_nt(dv_ref[...], w[2])
    x = x_ref[...].astype(F32)
    r1 = rms_factor(x)
    scaled = dn * gain_ref[...]
    dgain_ref[...] += jnp.sum(dn * x * r1, axis=0, keepdims=True)
    gt_ref[...] = (
        gm_ref[...]
        + r1 * scaled
        - x * (r1 * r1 * r1 * jnp.mean(scaled * x, axis=-1, keepdims=True))
    )


def input_call(me, x, gain, gm, dq, dk, dv, blocks, rows, tile):
    nd, (count, width) = len(blocks), x.shape
    row_spec = pl.BlockSpec((tile, width), lambda i: (i, 0))
    whole = lambda *shape: pl.BlockSpec(shape, lambda i: (0,) * len(shape))
    return pl.pallas_call(
        lambda *refs: input_kernel(nd, rows, *refs),
        grid=(count // tile,),
        in_specs=[SMEM, row_spec, whole(1, width)] + [row_spec] * 4 + [ANY] * nd,
        out_specs=[row_spec, whole(1, width)],
        out_shape=[
            jax.ShapeDtypeStruct((count, width), F32),
            jax.ShapeDtypeStruct((1, width), F32),
        ],
        scratch_shapes=[
            pltpu.VMEM((3, width, width), BF16),
            pltpu.SemaphoreType.DMA((3, nd)),
        ],
        compiler_params=params(),
        cost_estimate=cost(6 * count * width * width, 16 * count * width + 6 * width * width),
        name="input_grad",
    )(me, x, gain, gm, dq, dk, dv, *blocks)


def after(value, *earlier):
    return lax.optimization_barrier((value, *earlier))[0]


class Moves:
    def __init__(self, nd, nw):
        self.nd, self.nw = nd, nw
        self.yn = nd // 2
        self.xn = self.yn if nw % self.yn == 0 else 1
        self.zn = nw // self.xn

    def send(self, value, axis, k):
        if axis in ("core", "y"):
            flip = k if axis == "core" else 2 * k
            return lax.ppermute(value, "dp", [(i, i ^ flip) for i in range(self.nd)])
        flip = k if axis == "x" else self.xn * k
        return lax.ppermute(value, "wide", [(i, i ^ flip) for i in range(self.nw)])

    def where(self, axis):
        if axis == "y":
            return lax.axis_index("dp") // 2
        if axis == "x":
            return lax.axis_index("wide") % self.xn
        return lax.axis_index("wide") // self.xn


def by_distance(parts, place):
    parts = list(parts)
    bit = 1
    while bit < len(parts):
        on = (place & bit) != 0
        parts = [jnp.where(on, parts[i ^ bit], parts[i]) for i in range(len(parts))]
        bit *= 2
    return parts


def cut(value, count, axis):
    size = value.shape[axis] // count
    return [lax.slice_in_dim(value, i * size, (i + 1) * size, axis=axis) for i in range(count)]


def summed(values):
    total = values[0].astype(F32)
    for v in values[1:]:
        total = total + v.astype(F32)
    return total


def scatter_dp(moves, their, mine):
    got = moves.send(their, "core", 1)
    parts = [mine[0], got[0]]
    for kk in range(1, moves.yn):
        parts.append(moves.send(summed([mine[kk], got[kk]]).astype(BF16), "y", kk))
    return summed(parts)


def sum_wide(moves, part):
    px, pz = moves.where("x"), moves.where("z")
    cols = by_distance(cut(part, moves.xn, 1), px)
    kept = [cols[0]] + [moves.send(cols[k].astype(BF16), "x", k) for k in range(1, moves.xn)]
    rows = by_distance(cut(summed(kept), moves.zn, 0), pz)
    kept = [rows[0]] + [moves.send(rows[k].astype(BF16), "z", k) for k in range(1, moves.zn)]
    block = summed(kept).astype(BF16)
    rows = [block] + [moves.send(block, "z", k) for k in range(1, moves.zn)]
    strip = jnp.concatenate(by_distance(rows, pz), axis=0)
    cols = [strip] + [moves.send(strip, "x", k) for k in range(1, moves.xn)]
    return jnp.concatenate(by_distance(cols, px), axis=1).astype(F32)


def gather_dp(moves, shard, earlier=None):
    out = []
    for kk in range(moves.yn):
        far = shard if kk == 0 else moves.send(shard, "y", kk)
        out += [far, moves.send(far, "core", 1)]
    return out


def gather_dp_halves(moves, shard, earlier):
    if moves.yn != 2 or moves.xn != 2:
        return gather_dp(moves, shard)
    px = moves.where("x")
    half = by_distance(cut(shard, 2, 0), px)[0]
    near = moves.send(after(half, earlier), "y", 1)
    far = moves.send(near, "x", 1)
    other = jnp.concatenate(by_distance([near, far], px), axis=0)
    return [shard, moves.send(shard, "core", 1), other, moves.send(other, "core", 1)]


def slot_rank(owners):
    same_owner = owners[:, None] == owners[None, :]
    ids = jnp.arange(owners.shape[0])
    return jnp.sum((same_owner & (ids[None, :] < ids[:, None])).astype(jnp.int32), axis=1)


def shards(
    tokens,
    lengths,
    indices,
    memory_table,
    w_query,
    w_key,
    w_value,
    w_out,
    w_in,
    w_back,
    gain_one,
    gain_two,
    rel_bias,
    cotangent,
):
    nd, nw = lax.axis_size("dp"), lax.axis_size("wide")
    moves = Moves(nd, nw)
    dp_index = lax.axis_index("dp")
    me = dp_index.astype(jnp.int32).reshape(1)
    quest = lengths.shape[0]
    count, width = tokens.shape
    rows = w_query.shape[0]
    entries = memory_table.shape[0]
    per_dev = quest * TOPK
    capacity = (per_dev + nw - 1) // nw + 1
    slots = nw * capacity

    flat = indices.reshape(per_dev)
    owner = flat // entries
    rank = slot_rank(owner)
    local = flat - owner * entries
    hit = (owner[None, None, :] == jnp.arange(nw)[:, None, None]) & (
        rank[None, None, :] == jnp.arange(LANES)[None, :, None]
    )
    request = jnp.sum(jnp.where(hit, local[None, None, :] + 1, 0), axis=2) - 1
    asked = lax.all_to_all(request, "wide", 0, 0, tiled=True)
    asked = asked[:, :capacity].reshape(slots)

    small = jnp.concatenate(
        [gain_one, gain_two, rel_bias.reshape(-1)]
    )
    small = jnp.pad(small, (0, 16 * width - small.shape[0])).reshape(16, width)
    packed = jnp.concatenate([w_query, w_key, w_value, w_out, small], axis=0)
    square = gather_dp(moves, packed)
    ins = gather_dp_halves(moves, w_in, square[2])
    backs = gather_dp_halves(moves, w_back, ins[2])

    selection = (asked[:, None] == jnp.arange(entries)[None, :]).astype(BF16)
    outgoing = jnp.dot(selection, memory_table, preferred_element_type=F32).astype(BF16)
    incoming = lax.all_to_all(
        outgoing.reshape(nw, capacity, 4 * width), "wide", 0, 0, tiled=True
    ).reshape(slots, 4 * width)
    slot = (owner * capacity + rank).reshape(quest, TOPK)
    slot = jnp.pad(slot, ((0, 0), (0, PADK - TOPK)), constant_values=-1).reshape(quest * PADK)
    slot_hot = (slot[:, None] == jnp.arange(slots)[None, :]).astype(BF16)
    prefix = jnp.dot(slot_hot, incoming, preferred_element_type=F32).astype(BF16)

    rows_asked = asked
    rows_asked = jnp.stack([rows_asked, moves.send(rows_asked, "core", 1)])
    rows_asked = jnp.stack(
        [rows_asked] + [moves.send(rows_asked, "y", kk) for kk in range(1, moves.yn)]
    ).reshape(nd * slots)

    smalls = jnp.stack([block[4 * rows :].reshape(-1) for block in square])
    smalls = jnp.take(smalls, jnp.arange(nd) ^ dp_index, axis=0).astype(F32)
    full_gain_one = smalls[:, :rows].reshape(1, width)
    full_gain_two = smalls[:, rows : 2 * rows].reshape(1, width)
    bias_size = rel_bias.size
    full_bias = smalls[:, 2 * rows : 2 * rows + bias_size].reshape(NB, HEADS)
    onehot = np.zeros((QLEN, LANES, NB), np.float32)
    onehot[:, :QLEN] = bucket_table(QLEN, NB, MAXDIST)
    onehot = onehot.reshape(QLEN * LANES, NB)
    bias = jnp.dot(
        full_bias.T.astype(BF16), jnp.asarray(onehot.T, BF16), preferred_element_type=F32
    ).reshape(HEADS * QLEN, LANES)

    tile = 4 * QLEN
    q, k, v, normed = qkv_call(me, tokens, full_gain_one, square, rows, tile)
    probs, ctx, mid, n2 = attn_call(
        me, lengths, q, k, v, prefix, tokens, bias, full_gain_two, square, rows, 4
    )
    layer_out, dn2, back_their, back_mine, in_their, in_mine = ff_call(
        me, n2, mid, cotangent, ins, backs, tile
    )
    grad_back = sum_wide(moves, scatter_dp(moves, back_their, back_mine))
    grad_in = sum_wide(moves, scatter_dp(moves, in_their, in_mine))

    gm, gml, dq, dk, dv, dpre, dbias, dgain_two = attn_back_call(
        me, cotangent, dn2, mid, full_gain_two, probs, q, k, v, prefix, square, rows, 4
    )
    sq_their, sq_mine = square_call(me, nd, rows, normed, ctx, dq, dk, dv, gml)
    grad_square = sum_wide(moves, scatter_dp(moves, sq_their, sq_mine))

    returned = mm_tn(slot_hot, dpre).astype(BF16)
    arrived = lax.all_to_all(
        returned.reshape(nw, capacity, 4 * width), "wide", 0, 0, tiled=True
    ).reshape(slots, nd, 4 * width // nd)
    cols = by_distance([arrived[:, j] for j in range(nd)], dp_index)
    got = moves.send(jnp.stack(cols[1::2]), "core", 1)
    pairs = [jnp.concatenate([cols[2 * kk], got[kk]], axis=0) for kk in range(moves.yn)]
    table_rows = jnp.concatenate(
        [pairs[0]] + [moves.send(pairs[kk], "y", kk) for kk in range(1, moves.yn)], axis=0
    )
    scatter = (jnp.arange(entries)[:, None] == rows_asked[None, :]).astype(BF16)
    grad_table = jnp.dot(scatter, table_rows, preferred_element_type=F32)

    grad_tokens, dgain_one = input_call(
        me, tokens, full_gain_one, gm, dq, dk, dv, square, rows, tile
    )
    bucket_sums = jnp.dot(
        jnp.asarray(onehot.T), dbias.reshape(HEADS, QLEN * LANES).T, precision=lax.Precision.HIGHEST
    )
    small_sums = lax.psum(
        jnp.concatenate([dgain_one[0], dgain_two[0], bucket_sums.reshape(-1)]), ("dp", "wide")
    )
    own = lambda vec, size: lax.dynamic_slice_in_dim(vec, dp_index * size, size)
    grad_gain_one = own(small_sums[:width], rows)
    grad_gain_two = own(small_sums[width : 2 * width], rows)
    grad_bias = own(small_sums[2 * width :].reshape(NB, HEADS), NB // nd)
    return (
        layer_out,
        grad_tokens,
        grad_square[:rows],
        grad_square[rows : 2 * rows],
        grad_square[2 * rows : 3 * rows],
        grad_square[3 * rows :],
        grad_in,
        grad_back,
        grad_gain_one,
        grad_gain_two,
        grad_bias,
        grad_table,
    )


def solution(mesh):
    split = P(("dp", "wide"), None)
    weight = P("dp", None)
    return jax.shard_map(
        shards,
        mesh=mesh,
        in_specs=(split, P(("dp", "wide")), split, P("wide", None))
        + (weight,) * 6
        + (P("dp"), P("dp"), weight, split),
        out_specs=(split, split) + (weight,) * 6 + (P("dp"), P("dp"), weight, P("wide", "dp")),
        check_vma=False,
    )
```

```python
import math

import jax
import jax.numpy as jnp
import numpy as np
from jax import lax
from jax.experimental import pallas as pl
from jax.experimental.pallas import tpu as pltpu
from jax.sharding import PartitionSpec as P

HEADS = 12
HD = 64
NB = 32
MAXDIST = 128
QLEN = 64
TOPK = 10
PADK = 16
LANES = 128
QUAD = 256
EXTRA = 64
EPS = 1e-06
F32 = jnp.float32
BF16 = jnp.bfloat16
VMEM_BYTES = 58 * 1024 * 1024
ANY = pl.BlockSpec(memory_space=pl.ANY)
SMEM = pl.BlockSpec(memory_space=pltpu.SMEM)


def bucket_table(length, buckets, max_reach):
    half_count = buckets // 2
    near_count = half_count // 2
    onehot = np.zeros((length, length, buckets), np.float32)
    for target in range(length):
        for source in range(length):
            offset = source - target
            bucket = half_count if offset > 0 else 0
            distance = abs(offset)
            if distance < near_count:
                bucket += distance
            else:
                bucket += min(
                    half_count - 1,
                    near_count
                    + int(
                        math.log(distance / near_count)
                        / math.log(max_reach / near_count)
                        * (half_count - near_count)
                    ),
                )
            onehot[target, source, bucket] = 1.0
    return onehot


def mm(a, b):
    return jnp.dot(a, b, preferred_element_type=F32)


def mm_nt(a, b):
    return lax.dot_general(a, b, (((1,), (1,)), ((), ())), preferred_element_type=F32)


def mm_tn(a, b):
    return lax.dot_general(a, b, (((0,), (0,)), ((), ())), preferred_element_type=F32)


def cost(flops, scale, size):
    return pl.CostEstimate(flops=int(scale * flops), bytes_accessed=int(size), transcendentals=0)


def params(grid=True):
    return pltpu.CompilerParams(
        vmem_limit_bytes=VMEM_BYTES,
        **(dict(dimension_semantics=("arbitrary",)) if grid else {}),
    )


def rms_factor(values):
    return lax.rsqrt(jnp.mean(values * values, axis=-1, keepdims=True) + EPS)


def block_copies(member, blocks, first, rows, target, sems):
    return [
        pltpu.make_async_copy(
            block.at[pl.ds(first, rows)],
            target.at[pl.ds(pl.multiple_of((member ^ k) * rows, rows), rows)],
            sems.at[k],
        )
        for k, block in enumerate(blocks)
    ]


def pack_kernel(*refs):
    (q_ref, k_ref, v_ref, o_ref, one_ref, two_ref, bias_ref, out_ref, small) = refs
    rows = q_ref.shape[0]
    for i, ref in enumerate((q_ref, k_ref, v_ref, o_ref)):
        out_ref[i * rows : (i + 1) * rows, :] = ref[...]
    small[...] = jnp.zeros_like(small)
    small[0:1, :rows] = one_ref[...].astype(F32)
    small[1:2, :rows] = two_ref[...].astype(F32)
    small[8 : 8 + bias_ref.shape[0], : bias_ref.shape[1]] = bias_ref[...].astype(F32)
    out_ref[4 * rows :, :] = small[...].astype(BF16)


def pack_call(squares, gain_one, gain_two, rel_bias):
    rows, width = squares[0].shape
    vmem = pl.BlockSpec(memory_space=pltpu.VMEM)
    return pl.pallas_call(
        pack_kernel,
        in_specs=[vmem] * 7,
        out_specs=vmem,
        out_shape=jax.ShapeDtypeStruct((4 * rows + PADK, width), BF16),
        scratch_shapes=[pltpu.VMEM((PADK, width), F32)],
        compiler_params=params(False),
        cost_estimate=cost(0, 1, 16 * rows * width),
        name="pack",
    )(*squares, gain_one.reshape(1, -1), gain_two.reshape(1, -1), rel_bias)


def qkv_kernel(nd, rows, me, x_ref, gain_ref, *rest):
    blocks, (q_ref, k_ref, v_ref, n_ref, w, sems) = rest[:nd], rest[nd:]

    @pl.when(pl.program_id(0) == 0)
    def _():
        copies = []
        for i in range(3):
            copies += block_copies(me[0], blocks, i * rows, rows, w.at[i], sems.at[i])
        for c in copies:
            c.start()
        for c in copies:
            c.wait()

    x = x_ref[...].astype(F32)
    normed = (x * rms_factor(x) * gain_ref[...]).astype(BF16)
    n_ref[...] = normed
    for i, out in enumerate((q_ref, k_ref, v_ref)):
        out[...] = mm(normed, w[i]).astype(BF16)


def qkv_call(me, x, gain, blocks, rows, tile):
    nd, (count, width) = len(blocks), x.shape
    row_spec = pl.BlockSpec((tile, width), lambda i: (i, 0))
    return pl.pallas_call(
        lambda *refs: qkv_kernel(nd, rows, *refs),
        grid=(count // tile,),
        in_specs=[SMEM, row_spec, pl.BlockSpec((1, width), lambda i: (0, 0))] + [ANY] * nd,
        out_specs=[row_spec] * 4,
        out_shape=[jax.ShapeDtypeStruct((count, width), BF16)] * 4,
        scratch_shapes=[
            pltpu.VMEM((3, width, width), BF16),
            pltpu.SemaphoreType.DMA((3, nd)),
        ],
        compiler_params=params(),
        cost_estimate=cost(6 * count * width * width, 2.9, 10 * count * width + 6 * width * width),
        name="norm_qkv",
    )(me, x, gain, *blocks)


def key_list(tok, pre, first):
    width = tok.shape[1]
    return jnp.concatenate(
        [
            tok,
            pre[:, first * width : (first + 1) * width],
            pre[:, (first + 1) * width : (first + 2) * width],
            jnp.zeros((LANES - QLEN - 2 * PADK, width), tok.dtype),
        ],
        axis=0,
    )


def spread_heads(part):
    head = lax.broadcasted_iota(jnp.int32, part.shape, 1) // HD
    return jnp.concatenate(
        [jnp.where(head == h, part, jnp.zeros_like(part)) for h in range(QUAD // HD)], axis=0
    )


def gather_heads(full):
    head = lax.broadcasted_iota(jnp.int32, (QLEN, QUAD), 1) // HD
    out = full[:QLEN]
    for h in range(1, QUAD // HD):
        out = jnp.where(head == h, full[h * QLEN : (h + 1) * QLEN], out)
    return out


def attn_kernel(nd, rows, batch, me, lens, *rest):
    (q_ref, k_ref, v_ref, pre_ref, x_ref, bias_ref, gain_ref) = rest[:7]
    blocks = rest[7 : 7 + nd]
    (p_ref, ctx_ref, mid_ref, n2_ref, w, sems) = rest[7 + nd :]
    step = pl.program_id(0)

    @pl.when(step == 0)
    def _():
        copies = block_copies(me[0], blocks, 3 * rows, rows, w, sems)
        for c in copies:
            c.start()
        for c in copies:
            c.wait()

    lane = lax.broadcasted_iota(jnp.int32, (1, LANES), 1)
    fixed = ((lane >= QLEN) & (lane < QLEN + TOPK)) | (
        (lane >= QLEN + PADK) & (lane < QLEN + PADK + TOPK)
    )
    width = q_ref.shape[1]
    for b in range(batch):
        r = slice(b * QLEN, (b + 1) * QLEN)
        pre = pre_ref[b * PADK : (b + 1) * PADK, :]
        keys = key_list(k_ref[r, :], pre, 0)
        values = key_list(v_ref[r, :], pre, 2)
        valid = fixed | (lane < jnp.minimum(lens[step * batch + b], QLEN))
        for t in range(width // QUAD):
            c = slice(t * QUAD, (t + 1) * QUAD)
            scores = mm_nt(spread_heads(q_ref[r, c]), keys[:, c]) + bias_ref[c, :]
            scores = jnp.where(valid, scores, -1e9)
            e = jnp.exp(scores - jnp.max(scores, axis=1, keepdims=True))
            probs = (e * (1.0 / jnp.sum(e, axis=1, keepdims=True))).astype(BF16)
            p_ref[b, c, :] = probs
            ctx_ref[r, c] = gather_heads(mm(probs, values[:, c])).astype(BF16)
    middle = x_ref[...].astype(F32) + mm(ctx_ref[...], w[...])
    mid_ref[...] = middle
    n2_ref[...] = (middle * rms_factor(middle) * gain_ref[...]).astype(BF16)


def attn_call(me, lens, q, k, v, prefix, x, bias, gain, blocks, rows, batch):
    nd, (count, width) = len(blocks), q.shape
    tile = batch * QLEN
    row_spec = pl.BlockSpec((tile, width), lambda i: (i, 0))
    whole = lambda shape: pl.BlockSpec(shape, lambda i: (0,) * len(shape))
    quest = count // QLEN
    return pl.pallas_call(
        lambda *refs: attn_kernel(nd, rows, batch, *refs),
        grid=(count // tile,),
        in_specs=[SMEM, SMEM, row_spec, row_spec, row_spec]
        + [
            pl.BlockSpec((batch * PADK, prefix.shape[1]), lambda i: (i, 0)),
            row_spec,
            whole(bias.shape),
            whole((1, width)),
        ]
        + [ANY] * nd,
        out_specs=[
            pl.BlockSpec((batch, HEADS * QLEN, LANES), lambda i: (i, 0, 0)),
            row_spec,
            row_spec,
            row_spec,
        ],
        out_shape=[
            jax.ShapeDtypeStruct((quest, HEADS * QLEN, LANES), BF16),
            jax.ShapeDtypeStruct((count, width), BF16),
            jax.ShapeDtypeStruct((count, width), F32),
            jax.ShapeDtypeStruct((count, width), BF16),
        ],
        scratch_shapes=[pltpu.VMEM((width, width), BF16), pltpu.SemaphoreType.DMA((nd,))],
        compiler_params=params(),
        cost_estimate=cost(12 * count * width * width, 2.4, 20 * count * width),
        name="attention",
    )(me, lens, q, k, v, prefix, x, bias, gain, *blocks)


def ff_order(nd):
    return list(range(1, nd, 2)) + list(range(0, nd, 2))


def rel_of(step, half):
    return jnp.where(step < half, 2 * step + 1, 2 * (step - half))


def ff_kernel(nd, rows, tile, me, n2_ref, mid_ref, g_ref, *rest):
    in_blocks, back_blocks = rest[:nd], rest[nd : 2 * nd]
    (out_ref, dn2_ref, bt_ref, bm_ref, gh_ref) = rest[2 * nd : 2 * nd + 5]
    (win, wback, act, total, h0, h1, d0, d1, in_sems, back_sems) = rest[2 * nd + 5 :]
    step = pl.program_id(0)
    half = nd // 2
    member = me[0]
    count, width = n2_ref.shape
    chunk = wback.shape[1]
    root = math.sqrt(2 / math.pi)
    cube = root * 0.044715

    @pl.when(step == 0)
    def _():
        copies = block_copies(member, in_blocks, 0, rows, win, in_sems)
        for s, k in enumerate(ff_order(nd)):
            copies.append(pltpu.make_async_copy(back_blocks[k], wback.at[s], back_sems.at[s]))
        for c in copies:
            c.start()
        total[...] = mid_ref[...]
        dn2_ref[...] = jnp.zeros_like(dn2_ref)
        for c in copies:
            c.wait()

    cols = pl.ds(pl.multiple_of((member ^ rel_of(step, half)) * chunk, LANES), chunk)
    w_in = win[:, cols]
    w_back = wback[step]
    hs, ds = (h0, h1), (d0, d1)
    tiles = count // tile
    for m in range(tiles + 1):
        if m < tiles:
            r = slice(m * tile, (m + 1) * tile)
            hs[m % 2][...] = mm(n2_ref[r, :], w_in)
            ds[m % 2][...] = mm_nt(g_ref[r, :], w_back)
        if m > 0:
            r = slice((m - 1) * tile, m * tile)
            h = hs[(m - 1) % 2][...]
            h2 = h * h
            p = 0.5 + 0.5 * jnp.tanh(h * (root + cube * h2))
            a = (h * p).astype(BF16)
            slope = p * (1.0 + (1.0 - p) * (h * (2 * root + 6 * cube * h2)))
            d = (ds[(m - 1) % 2][...] * slope).astype(BF16)
            act[r, :] = a
            gh_ref[0, r, :] = d
            total[r, :] += mm(a, w_back)
            dn2_ref[r, :] += mm_nt(d, w_in)

    @pl.when(step < half)
    def _():
        bt_ref[...] = mm_tn(act[...], g_ref[...]).astype(BF16)[None]

    @pl.when(step >= half)
    def _():
        bm_ref[...] = mm_tn(act[...], g_ref[...]).astype(BF16)[None]

    @pl.when(step == nd - 1)
    def _():
        out_ref[...] = total[...].astype(BF16)


def ff_call(me, n2, mid, g, in_blocks, back_blocks, tile):
    nd, (count, width) = len(in_blocks), n2.shape
    half = nd // 2
    rows, hidden = in_blocks[0].shape
    chunk = back_blocks[0].shape[0]
    whole = lambda *shape: pl.BlockSpec(shape, lambda i: (0,) * len(shape))
    return pl.pallas_call(
        lambda *refs: ff_kernel(nd, rows, tile, *refs),
        grid=(nd,),
        in_specs=[SMEM] + [whole(count, width)] * 3 + [ANY] * (2 * nd),
        out_specs=[
            whole(count, width),
            whole(count, width),
            pl.BlockSpec((1, chunk, width), lambda i: (jnp.minimum(i, half - 1), 0, 0)),
            pl.BlockSpec((1, chunk, width), lambda i: (jnp.maximum(i - half, 0), 0, 0)),
            pl.BlockSpec((1, count, chunk), lambda i: (i, 0, 0)),
        ],
        out_shape=[
            jax.ShapeDtypeStruct((count, width), BF16),
            jax.ShapeDtypeStruct((count, width), F32),
            jax.ShapeDtypeStruct((half, chunk, width), BF16),
            jax.ShapeDtypeStruct((half, chunk, width), BF16),
            jax.ShapeDtypeStruct((nd, count, chunk), BF16),
        ],
        scratch_shapes=[
            pltpu.VMEM((width, hidden), BF16),
            pltpu.VMEM((nd, chunk, width), BF16),
            pltpu.VMEM((count, chunk), BF16),
            pltpu.VMEM((count, width), F32),
        ]
        + [pltpu.VMEM((tile, chunk), F32)] * 4
        + [pltpu.SemaphoreType.DMA((nd,)), pltpu.SemaphoreType.DMA((nd,))],
        compiler_params=params(),
        cost_estimate=cost(10 * count * width * hidden, 1.8, 20 * count * width + 6 * width * hidden),
        name="feed_forward",
    )(me, n2, mid, g, *in_blocks, *back_blocks)


def ff_in_kernel(nd, rows, me, n2_ref, gh_ref, it_ref, im_ref, gin):
    step = pl.program_id(0)
    chunk = gh_ref.shape[2]
    at = (me[0] ^ rel_of(step, nd // 2)) * chunk
    gin[:, pl.ds(pl.multiple_of(at, LANES), chunk)] = mm_tn(n2_ref[...], gh_ref[0]).astype(BF16)

    @pl.when(step == nd - 1)
    def _():
        width = n2_ref.shape[1]
        for kk in range(nd // 2):
            for ref, k in ((it_ref, 2 * kk + 1), (im_ref, 2 * kk)):
                at = pl.ds(pl.multiple_of((me[0] ^ k) * rows, rows), rows)
                for j in range(nd * chunk // width):
                    ref[kk, j * rows : (j + 1) * rows, :] = gin[at, j * width : (j + 1) * width]


def ff_in_call(me, n2, gh, rows):
    (count, width), (nd, _, chunk) = n2.shape, gh.shape
    whole = lambda *shape: pl.BlockSpec(shape, lambda i: (0,) * len(shape))
    shape = (nd // 2, rows * nd * chunk // width, width)
    return pl.pallas_call(
        lambda *refs: ff_in_kernel(nd, rows, *refs),
        grid=(nd,),
        in_specs=[SMEM, whole(count, width), pl.BlockSpec((1, count, chunk), lambda i: (i, 0, 0))],
        out_specs=[whole(*shape)] * 2,
        out_shape=[jax.ShapeDtypeStruct(shape, BF16)] * 2,
        scratch_shapes=[pltpu.VMEM((width, nd * chunk), BF16)],
        compiler_params=params(),
        cost_estimate=cost(2 * count * width * nd * chunk, 2.4, 2 * nd * chunk * (count + width)),
        name="feed_forward_in",
    )(me, n2, gh)


def mid_kernel(nd, rows, me, g_ref, dn2_ref, mid_ref, gain_ref, *rest):
    blocks, (gm_ref, gml_ref, dctx_ref, w, sems) = rest[:nd], rest[nd:]

    @pl.when(pl.program_id(0) == 0)
    def _():
        copies = block_copies(me[0], blocks, 3 * rows, rows, w, sems)
        for c in copies:
            c.start()
        for c in copies:
            c.wait()

    mid, dn2 = mid_ref[...], dn2_ref[...]
    r2 = rms_factor(mid)
    scaled = dn2 * gain_ref[...]
    gm = (
        g_ref[...].astype(F32)
        + r2 * scaled
        - mid * (r2 * r2 * r2 * jnp.mean(scaled * mid, axis=-1, keepdims=True))
    )
    gm_ref[...] = gm
    low = gm.astype(BF16)
    gml_ref[...] = low
    dctx_ref[...] = mm_nt(low, w[...]).astype(BF16)


def mid_call(me, g, dn2, mid, gain, blocks, rows, tile):
    nd, (count, width) = len(blocks), g.shape
    row_spec = pl.BlockSpec((tile, width), lambda i: (i, 0))
    whole = pl.BlockSpec((1, width), lambda i: (0, 0))
    rows_of = lambda dtype: jax.ShapeDtypeStruct((count, width), dtype)
    return pl.pallas_call(
        lambda *refs: mid_kernel(nd, rows, *refs),
        grid=(count // tile,),
        in_specs=[SMEM] + [row_spec] * 3 + [whole] + [ANY] * nd,
        out_specs=[row_spec] * 3,
        out_shape=[rows_of(F32), rows_of(BF16), rows_of(BF16)],
        scratch_shapes=[pltpu.VMEM((width, width), BF16), pltpu.SemaphoreType.DMA((nd,))],
        compiler_params=params(),
        cost_estimate=cost(4 * count * width * width, 4.0, 18 * count * width),
        name="norm_back",
    )(me, g, dn2, mid, gain, *blocks)


def attn_back_kernel(batch, *refs):
    (dctx_ref, p_ref, q_ref, k_ref, v_ref, pre_ref) = refs[:6]
    (dq_ref, dk_ref, dv_ref, dpre_ref, dbias_ref) = refs[6:]

    @pl.when(pl.program_id(0) == 0)
    def _():
        dbias_ref[...] = jnp.zeros_like(dbias_ref)

    width = q_ref.shape[1]
    for b in range(batch):
        r = slice(b * QLEN, (b + 1) * QLEN)
        pr = slice(b * PADK, (b + 1) * PADK)
        pre = pre_ref[pr, :]
        keys = key_list(k_ref[r, :], pre, 0)
        values = key_list(v_ref[r, :], pre, 2)
        for t in range(width // QUAD):
            c = slice(t * QUAD, (t + 1) * QUAD)
            gs = spread_heads(dctx_ref[r, c])
            qs = spread_heads(q_ref[r, c])
            low_probs = p_ref[b, c, :]
            probs = low_probs.astype(F32)
            gp = mm_nt(gs, values[:, c])
            dval = mm_tn(low_probs, gs)
            ds = (probs * (gp - jnp.sum(probs * gp, axis=1, keepdims=True))).astype(BF16)
            dbias_ref[c, :] += ds.astype(F32)
            dq_ref[r, c] = gather_heads(mm(ds, keys[:, c])).astype(BF16)
            dkey = mm_tn(ds, qs)
            for ref, first, grad in ((dk_ref, 0, dkey), (dv_ref, 2, dval)):
                low_grad = grad.astype(BF16)
                ref[r, c] = low_grad[:QLEN]
                for s in range(2):
                    at = (first + s) * width + t * QUAD
                    dpre_ref[pr, at : at + QUAD] = low_grad[
                        QLEN + s * PADK : QLEN + (s + 1) * PADK
                    ]


def attn_back_call(dctx, probs, q, k, v, prefix, batch):
    count, width = q.shape
    tile = batch * QLEN
    row_spec = pl.BlockSpec((tile, width), lambda i: (i, 0))
    pre_spec = pl.BlockSpec((batch * PADK, prefix.shape[1]), lambda i: (i, 0))
    rows_of = jax.ShapeDtypeStruct((count, width), BF16)
    return pl.pallas_call(
        lambda *refs: attn_back_kernel(batch, *refs),
        grid=(count // tile,),
        in_specs=[row_spec, pl.BlockSpec((batch, HEADS * QLEN, LANES), lambda i: (i, 0, 0))]
        + [row_spec] * 3
        + [pre_spec],
        out_specs=[row_spec] * 3
        + [pre_spec, pl.BlockSpec((HEADS * QLEN, LANES), lambda i: (0, 0))],
        out_shape=[rows_of] * 3
        + [
            jax.ShapeDtypeStruct(prefix.shape, BF16),
            jax.ShapeDtypeStruct((HEADS * QLEN, LANES), F32),
        ],
        compiler_params=params(),
        cost_estimate=cost(20 * count * width * width, 1.9, 20 * count * width),
        name="attention_back",
    )(dctx, probs, q, k, v, prefix)


def square_kernel(nd, rows, pairs, extra, me, *refs):
    ins, (their, mine, full) = refs[: -3], refs[-3:]
    for i in range(pairs):
        left, right = ins[2 * i], ins[2 * i + 1]
        width = left.shape[1]
        for c in range(0, width, QUAD):
            full[i, c : c + QUAD, :] = mm_tn(left[:, c : c + QUAD], right[...]).astype(BF16)
    for kk in range(nd // 2):
        for ref, k in ((their, 2 * kk + 1), (mine, 2 * kk)):
            at = pl.ds(pl.multiple_of((me[0] ^ k) * rows, rows), rows)
            for i in range(pairs):
                ref[kk, i * rows : (i + 1) * rows, :] = full[i, at, :]
            if extra:
                base = pairs * rows
                ref[kk, base : base + PADK, :] = ins[-1][me[0] ^ k]
                ref[kk, base + PADK :, :] = jnp.zeros((EXTRA - PADK, width), BF16)


def square_call(me, nd, rows, pairs, small=None):
    count, width = pairs[0][0].shape
    vmem = pl.BlockSpec(memory_space=pltpu.VMEM)
    size = len(pairs) * rows + (0 if small is None else EXTRA)
    shape = jax.ShapeDtypeStruct((nd // 2, size, width), BF16)
    ins = [v for pair in pairs for v in pair] + ([] if small is None else [small])
    return pl.pallas_call(
        lambda *refs: square_kernel(nd, rows, len(pairs), small is not None, *refs),
        in_specs=[SMEM] + [vmem] * len(ins),
        out_specs=[vmem] * 2,
        out_shape=[shape] * 2,
        scratch_shapes=[pltpu.VMEM((len(pairs), width, width), BF16)],
        compiler_params=params(False),
        cost_estimate=cost(
            2 * len(pairs) * count * width * width,
            3.0,
            len(pairs) * (4 * count * width + 2 * width * width),
        ),
        name="square_grads",
    )(me, *ins)


def input_kernel(nd, rows, me, x_ref, gain_ref, gm_ref, dq_ref, dk_ref, dv_ref, *rest):
    blocks, (gt_ref, w, sems) = rest[:nd], rest[nd:]

    @pl.when(pl.program_id(0) == 0)
    def _():
        copies = []
        for i in range(3):
            copies += block_copies(me[0], blocks, i * rows, rows, w.at[i], sems.at[i])
        for c in copies:
            c.start()
        for c in copies:
            c.wait()

    dn = mm_nt(dq_ref[...], w[0]) + mm_nt(dk_ref[...], w[1]) + mm_nt(dv_ref[...], w[2])
    x = x_ref[...].astype(F32)
    r1 = rms_factor(x)
    scaled = dn * gain_ref[...]
    gt_ref[...] = (
        gm_ref[...]
        + r1 * scaled
        - x * (r1 * r1 * r1 * jnp.mean(scaled * x, axis=-1, keepdims=True))
    )


def input_call(me, x, gain, gm, dq, dk, dv, blocks, rows, tile):
    nd, (count, width) = len(blocks), x.shape
    row_spec = pl.BlockSpec((tile, width), lambda i: (i, 0))
    whole = lambda *shape: pl.BlockSpec(shape, lambda i: (0,) * len(shape))
    return pl.pallas_call(
        lambda *refs: input_kernel(nd, rows, *refs),
        grid=(count // tile,),
        in_specs=[SMEM, row_spec, whole(1, width)] + [row_spec] * 4 + [ANY] * nd,
        out_specs=row_spec,
        out_shape=jax.ShapeDtypeStruct((count, width), F32),
        scratch_shapes=[
            pltpu.VMEM((3, width, width), BF16),
            pltpu.SemaphoreType.DMA((3, nd)),
        ],
        compiler_params=params(),
        cost_estimate=cost(6 * count * width * width, 3.5, 16 * count * width + 6 * width * width),
        name="input_grad",
    )(me, x, gain, gm, dq, dk, dv, *blocks)


def after(value, *earlier):
    return lax.optimization_barrier((value, *earlier))[0]


class Moves:
    def __init__(self, nd, nw):
        self.nd, self.nw = nd, nw
        self.yn = nd // 2
        self.xn = self.yn if nw % self.yn == 0 else 1
        self.zn = nw // self.xn
        self.bits = nw.bit_length() - 1

    def send(self, value, axis, k):
        if axis in ("core", "y"):
            flip = k if axis == "core" else 2 * k
            return lax.ppermute(value, "dp", [(i, i ^ flip) for i in range(self.nd)])
        flip = k if axis == "x" else self.xn * k
        return lax.ppermute(value, "wide", [(i, i ^ flip) for i in range(self.nw)])

    def where(self, axis):
        if axis == "y":
            return lax.axis_index("dp") // 2
        if axis == "x":
            return lax.axis_index("wide") % self.xn
        return lax.axis_index("wide") // self.xn


def by_distance(parts, place):
    parts = list(parts)
    bit = 1
    while bit < len(parts):
        on = (place & bit) != 0
        parts = [jnp.where(on, parts[i ^ bit], parts[i]) for i in range(len(parts))]
        bit *= 2
    return parts


def cut(value, count, axis):
    size = value.shape[axis] // count
    return [lax.slice_in_dim(value, i * size, (i + 1) * size, axis=axis) for i in range(count)]


def summed(values):
    total = values[0].astype(F32)
    for v in values[1:]:
        total = total + v.astype(F32)
    return total


def core_sum(moves, their, mine):
    return mine, moves.send(their, "core", 1)


def by_wide(moves, value):
    *lead, rows, cols = value.shape
    return value.reshape(*lead, moves.nw, rows // moves.nw, cols)


def halves(moves, value, bit):
    *lead, n, r, c = value.shape
    pair = value.reshape(*lead, n // 2, 2, r, c)
    low, high = pair[..., 0, :, :], pair[..., 1, :, :]
    on = ((lax.axis_index("wide") >> bit) & 1) != 0
    return jnp.where(on, high, low), jnp.where(on, low, high)


def send_wide(moves, value, bit):
    return lax.ppermute(value, "wide", [(i, i ^ (1 << bit)) for i in range(moves.nw)])


def gather_dp(moves, shard, y_after=()):
    out = []
    for kk in range(moves.yn):
        out.append(shard if kk == 0 else moves.send(after(shard, *y_after), "y", kk))
    return out


def share_cores(moves, blocks, *deps):
    out = []
    for block in blocks:
        out += [block, moves.send(after(block, *deps), "core", 1)]
    return out


def spread_wide(moves, value):
    r, c = value.shape
    value = value.reshape(1, r, c)
    for bit in reversed(range(moves.bits)):
        got = send_wide(moves, value, bit)
        on = ((lax.axis_index("wide") >> bit) & 1) != 0
        value = jnp.stack([jnp.where(on, got, value), jnp.where(on, value, got)], axis=1)
        value = value.reshape(-1, r, c)
    return value.reshape(-1, c)


def slot_rank(owners):
    same_owner = owners[:, None] == owners[None, :]
    ids = jnp.arange(owners.shape[0])
    return jnp.sum((same_owner & (ids[None, :] < ids[:, None])).astype(jnp.int32), axis=1)


def shards(
    tokens,
    lengths,
    indices,
    memory_table,
    w_query,
    w_key,
    w_value,
    w_out,
    w_in,
    w_back,
    gain_one,
    gain_two,
    rel_bias,
    cotangent,
):
    nd, nw = lax.axis_size("dp"), lax.axis_size("wide")
    moves = Moves(nd, nw)
    dp_index = lax.axis_index("dp")
    me = dp_index.astype(jnp.int32).reshape(1)
    quest = lengths.shape[0]
    count, width = tokens.shape
    rows = w_query.shape[0]
    entries = memory_table.shape[0]
    per_dev = quest * TOPK
    capacity = (per_dev + nw - 1) // nw + 1
    slots = nw * capacity

    flat = indices.reshape(per_dev)
    owner = flat // entries
    rank = slot_rank(owner)
    local = flat - owner * entries
    hit = (owner[None, None, :] == jnp.arange(nw)[:, None, None]) & (
        rank[None, None, :] == jnp.arange(LANES)[None, :, None]
    )
    request = jnp.sum(jnp.where(hit, local[None, None, :] + 1, 0), axis=2) - 1
    packed = pack_call((w_query, w_key, w_value, w_out), gain_one, gain_two, rel_bias)

    early = lengths.astype(F32)
    for _ in range(2):
        early = moves.send(early, "core", 1) + 1.0
    asked = lax.all_to_all(after(request, packed, early), "wide", 0, 0, tiled=True)
    asked = asked[:, :capacity].reshape(slots)
    selection = (asked[:, None] == jnp.arange(entries)[None, :]).astype(BF16)
    outgoing = jnp.dot(selection, memory_table, preferred_element_type=F32).astype(BF16)
    outgoing = outgoing.reshape(nw, capacity, 4 * width)
    incoming = lax.all_to_all(outgoing, "wide", 0, 0, tiled=True).reshape(slots, 4 * width)

    square = share_cores(moves, gather_dp(moves, packed))

    both = jnp.stack([asked, moves.send(after(asked, outgoing), "core", 1)])
    far_asked = [moves.send(both, "y", kk) for kk in range(1, moves.yn)]
    rows_asked = jnp.stack([both] + far_asked).reshape(nd * slots)

    smalls = jnp.stack([block[4 * rows :] for block in square])
    smalls = jnp.stack(by_distance([smalls[k] for k in range(nd)], dp_index)).astype(F32)
    full_gain_one = smalls[:, 0, :rows].reshape(1, width)
    full_gain_two = smalls[:, 1, :rows].reshape(1, width)
    bias_size = rel_bias.size
    full_bias = smalls[:, 8 : 8 + NB // nd, :HEADS].reshape(NB, HEADS)
    onehot = np.zeros((QLEN, LANES, NB), np.float32)
    onehot[:, :QLEN] = bucket_table(QLEN, NB, MAXDIST)
    onehot = onehot.reshape(QLEN * LANES, NB)
    bias = jnp.dot(
        full_bias.T.astype(BF16), jnp.asarray(onehot.T, BF16), preferred_element_type=F32
    ).reshape(HEADS * QLEN, LANES)

    tile = 4 * QLEN
    q, k, v, normed = qkv_call(me, tokens, full_gain_one, square, rows, tile)
    ins = gather_dp(moves, w_in, (square[2], outgoing))
    backs = gather_dp(moves, w_back, (square[2], outgoing))

    slot = (owner * capacity + rank).reshape(quest, TOPK)
    slot = jnp.pad(slot, ((0, 0), (0, PADK - TOPK)), constant_values=-1).reshape(quest * PADK)
    slot_hot = (slot[:, None] == jnp.arange(slots)[None, :]).astype(BF16)
    prefix = jnp.dot(
        slot_hot, after(incoming, q, bias, *far_asked), preferred_element_type=F32
    ).astype(BF16)

    probs, ctx, mid, n2 = attn_call(
        me, (early - 2.0).astype(jnp.int32), q, k, v, prefix, tokens, bias, full_gain_two, square, rows, 4
    )

    ins = share_cores(moves, ins, ctx)
    backs = share_cores(moves, backs, ctx)
    layer_out, dn2, back_their, back_mine, gh = ff_call(me, n2, mid, cotangent, ins, backs, tile)
    b_terms = core_sum(moves, back_their, back_mine)
    in_their, in_mine = ff_in_call(me, n2, gh, rows)
    b_far = [summed([t[kk] for t in b_terms]).astype(BF16) for kk in range(1, moves.yn)]
    b_near = [moves.send(value, "y", kk + 1) for kk, value in enumerate(b_far)]
    i_terms = core_sum(moves, in_their, in_mine)
    gm, gml, dctx = mid_call(
        me, cotangent, after(dn2, in_mine, *b_far), mid, full_gain_two, square, rows, tile
    )
    i_cut = [halves(moves, by_wide(moves, term), 0) for term in i_terms]
    i_keep = [c[0] for c in i_cut]
    i_send = after(summed([c[1] for c in i_cut]).astype(BF16), gm)
    i_got = send_wide(moves, i_send, 0)

    dq, dk, dv, dpre, dbias = attn_back_call(after(dctx, i_send), probs, q, k, v, prefix, 4)

    b_cut = [
        halves(moves, by_wide(moves, term), 0)
        for term in [t[0] for t in b_terms] + [after(v, dq) for v in b_near]
    ]
    b_keep = [c[0] for c in b_cut]
    b_send = summed([c[1] for c in b_cut]).astype(BF16)
    b_got = send_wide(moves, b_send, 0)
    i_terms = i_keep + [after(i_got, b_send)]
    i_far = [summed([term[kk] for term in i_terms]).astype(BF16) for kk in range(1, moves.yn)]
    i_near = [moves.send(v, "y", kk + 1) for kk, v in enumerate(i_far)]

    sums = jnp.dot(
        jnp.asarray(onehot.T), dbias.reshape(HEADS, QLEN * LANES).T, precision=lax.Precision.HIGHEST
    ).reshape(nd, bias_size).astype(BF16)
    sums = jnp.pad(sums, ((0, 0), (0, PADK * width - bias_size))).reshape(nd, PADK, width)
    s_their, s_mine = square_call(
        me, nd, rows, ((normed, dq), (normed, dk), (normed, dv), (after(ctx, *i_far), gml)), sums
    )
    s_terms = core_sum(moves, after(s_their, b_got, *i_near), s_mine)

    def wide_step(value, bit, *deps):
        keep, send = halves(moves, value, bit)
        send = after(send.astype(BF16), *deps)
        return keep + send_wide(moves, send, bit).astype(F32), send

    p_sum = jnp.stack(
        [summed(b_keep + [after(b_got, s_mine)]), summed([term[0] for term in i_terms] + i_near)]
    )
    s_far = [summed([t[kk] for t in s_terms]).astype(BF16) for kk in range(1, moves.yn)]
    s_near = [moves.send(value, "y", kk + 1) for kk, value in enumerate(s_far)]

    p_sum, p_sent = wide_step(p_sum, 1, *s_far)

    returned = mm_tn(slot_hot, after(dpre, p_sent)).astype(BF16)
    arrived = lax.all_to_all(
        returned.reshape(nw, capacity, 4 * width), "wide", 0, 0, tiled=True
    )
    for bit in range(2, moves.bits):
        p_sum, p_sent = wide_step(p_sum, bit, returned, *s_near)
    p_all = lax.all_gather(p_sum[:, 0].astype(BF16), "wide", axis=0)
    grad_back = p_all[:, 0].reshape(w_back.shape).astype(F32)
    grad_in = jnp.concatenate(
        cut(p_all[:, 1].reshape(-1, width), w_in.shape[1] // width, 0), axis=1
    ).astype(F32)

    grad_tokens = input_call(
        me, tokens, full_gain_one, after(gm, returned), dq, dk, dv, square, rows, tile
    )
    s_sum = by_wide(moves, summed([t[0] for t in s_terms] + s_near))
    s_sum, _ = wide_step(s_sum, 0, arrived, grad_tokens)
    for bit in range(1, moves.bits):
        s_sum, _ = wide_step(s_sum, bit)
    grad_square = spread_wide(moves, s_sum[0].astype(BF16)).astype(F32)

    arrived = arrived.reshape(slots, nd, 4 * width // nd)
    cols = by_distance([arrived[:, j] for j in range(nd)], dp_index)
    got = moves.send(jnp.stack(cols[1::2]), "core", 1)
    pairs = [jnp.concatenate([cols[2 * kk], got[kk]], axis=0) for kk in range(moves.yn)]
    table_rows = jnp.concatenate(
        [pairs[0]] + [moves.send(pairs[kk], "y", kk) for kk in range(1, moves.yn)], axis=0
    )
    scatter = (jnp.arange(entries)[:, None] == rows_asked[None, :]).astype(BF16)
    grad_table = jnp.dot(scatter, table_rows, preferred_element_type=F32)

    grad_query, grad_key, grad_value, grad_out = cut(grad_square[: 4 * rows], 4, 0)
    gain_grad = lambda gain, *pairs: sum(
        jnp.sum(weight.astype(F32) * grad, axis=1) for weight, grad in pairs
    ) / gain.astype(F32)
    return (
        layer_out,
        grad_tokens,
        grad_query,
        grad_key,
        grad_value,
        grad_out,
        grad_in,
        grad_back,
        gain_grad(gain_one, (w_query, grad_query), (w_key, grad_key), (w_value, grad_value)),
        gain_grad(gain_two, (w_in, grad_in)),
        grad_square[4 * rows].reshape(-1)[: NB // nd * HEADS].reshape(NB // nd, HEADS),
        grad_table,
    )


def solution(mesh):
    split = P(("dp", "wide"), None)
    weight = P("dp", None)
    return jax.shard_map(
        shards,
        mesh=mesh,
        in_specs=(split, P(("dp", "wide")), split, P("wide", None))
        + (weight,) * 6
        + (P("dp"), P("dp"), weight, split),
        out_specs=(split, split) + (weight,) * 6 + (P("dp"), P("dp"), weight, P("wide", "dp")),
        check_vma=False,
    )
```

```python
import math

import jax
import jax.numpy as jnp
import numpy as np
from jax import lax
from jax.experimental import pallas as pl
from jax.experimental.pallas import tpu as pltpu
from jax.sharding import PartitionSpec as P

HEADS = 12
HD = 64
NB = 32
MAXDIST = 128
QLEN = 64
TOPK = 10
PADK = 16
LANES = 128
QUAD = 256
EXTRA = 64
EPS = 1e-06
F32 = jnp.float32
BF16 = jnp.bfloat16
VMEM_BYTES = 58 * 1024 * 1024
ANY = pl.BlockSpec(memory_space=pl.ANY)
SMEM = pl.BlockSpec(memory_space=pltpu.SMEM)


def bucket_table(length, buckets, max_reach):
    half_count = buckets // 2
    near_count = half_count // 2
    onehot = np.zeros((length, length, buckets), np.float32)
    for target in range(length):
        for source in range(length):
            offset = source - target
            bucket = half_count if offset > 0 else 0
            distance = abs(offset)
            if distance < near_count:
                bucket += distance
            else:
                bucket += min(
                    half_count - 1,
                    near_count
                    + int(
                        math.log(distance / near_count)
                        / math.log(max_reach / near_count)
                        * (half_count - near_count)
                    ),
                )
            onehot[target, source, bucket] = 1.0
    return onehot


def mm(a, b):
    return jnp.dot(a, b, preferred_element_type=F32)


def mm_nt(a, b):
    return lax.dot_general(a, b, (((1,), (1,)), ((), ())), preferred_element_type=F32)


def mm_tn(a, b):
    return lax.dot_general(a, b, (((0,), (0,)), ((), ())), preferred_element_type=F32)


def cost(flops, scale, size):
    return pl.CostEstimate(flops=int(scale * flops), bytes_accessed=int(size), transcendentals=0)


def params(grid=True):
    return pltpu.CompilerParams(
        vmem_limit_bytes=VMEM_BYTES,
        **(dict(dimension_semantics=("arbitrary",)) if grid else {}),
    )


def rms_factor(values):
    return lax.rsqrt(jnp.mean(values * values, axis=-1, keepdims=True) + EPS)


def block_copies(member, blocks, first, rows, target, sems):
    return [
        pltpu.make_async_copy(
            block.at[pl.ds(first, rows)],
            target.at[pl.ds(pl.multiple_of((member ^ k) * rows, rows), rows)],
            sems.at[k],
        )
        for k, block in enumerate(blocks)
    ]


def pack_kernel(*refs):
    (q_ref, k_ref, v_ref, o_ref, one_ref, two_ref, bias_ref, out_ref, small) = refs
    rows = q_ref.shape[0]
    for i, ref in enumerate((q_ref, k_ref, v_ref, o_ref)):
        out_ref[i * rows : (i + 1) * rows, :] = ref[...]
    small[...] = jnp.zeros_like(small)
    small[0:1, :rows] = one_ref[...].astype(F32)
    small[1:2, :rows] = two_ref[...].astype(F32)
    small[8 : 8 + bias_ref.shape[0], : bias_ref.shape[1]] = bias_ref[...].astype(F32)
    out_ref[4 * rows :, :] = small[...].astype(BF16)


def pack_call(squares, gain_one, gain_two, rel_bias):
    rows, width = squares[0].shape
    vmem = pl.BlockSpec(memory_space=pltpu.VMEM)
    return pl.pallas_call(
        pack_kernel,
        in_specs=[vmem] * 7,
        out_specs=vmem,
        out_shape=jax.ShapeDtypeStruct((4 * rows + PADK, width), BF16),
        scratch_shapes=[pltpu.VMEM((PADK, width), F32)],
        compiler_params=params(False),
        cost_estimate=cost(0, 1, 16 * rows * width),
        name="pack",
    )(*squares, gain_one.reshape(1, -1), gain_two.reshape(1, -1), rel_bias)


def qkv_kernel(nd, rows, me, x_ref, gain_ref, *rest):
    blocks, (q_ref, k_ref, v_ref, n_ref, w, sems) = rest[:nd], rest[nd:]

    @pl.when(pl.program_id(0) == 0)
    def _():
        copies = []
        for i in range(3):
            copies += block_copies(me[0], blocks, i * rows, rows, w.at[i], sems.at[i])
        for c in copies:
            c.start()
        for c in copies:
            c.wait()

    x = x_ref[...].astype(F32)
    normed = (x * rms_factor(x) * gain_ref[...]).astype(BF16)
    n_ref[...] = normed
    for i, out in enumerate((q_ref, k_ref, v_ref)):
        out[...] = mm(normed, w[i]).astype(BF16)


def qkv_call(me, x, gain, blocks, rows, tile):
    nd, (count, width) = len(blocks), x.shape
    row_spec = pl.BlockSpec((tile, width), lambda i: (i, 0))
    return pl.pallas_call(
        lambda *refs: qkv_kernel(nd, rows, *refs),
        grid=(count // tile,),
        in_specs=[SMEM, row_spec, pl.BlockSpec((1, width), lambda i: (0, 0))] + [ANY] * nd,
        out_specs=[row_spec] * 4,
        out_shape=[jax.ShapeDtypeStruct((count, width), BF16)] * 4,
        scratch_shapes=[
            pltpu.VMEM((3, width, width), BF16),
            pltpu.SemaphoreType.DMA((3, nd)),
        ],
        compiler_params=params(),
        cost_estimate=cost(6 * count * width * width, 0.1, count * width + 6 * width * width),
        name="norm_qkv",
    )(me, x, gain, *blocks)


def key_list(tok, pre, first):
    width = tok.shape[1]
    return jnp.concatenate(
        [
            tok,
            pre[:, first * width : (first + 1) * width],
            pre[:, (first + 1) * width : (first + 2) * width],
            jnp.zeros((LANES - QLEN - 2 * PADK, width), tok.dtype),
        ],
        axis=0,
    )


def spread_heads(part):
    head = lax.broadcasted_iota(jnp.int32, part.shape, 1) // HD
    return jnp.concatenate(
        [jnp.where(head == h, part, jnp.zeros_like(part)) for h in range(QUAD // HD)], axis=0
    )


def gather_heads(full):
    head = lax.broadcasted_iota(jnp.int32, (QLEN, QUAD), 1) // HD
    out = full[:QLEN]
    for h in range(1, QUAD // HD):
        out = jnp.where(head == h, full[h * QLEN : (h + 1) * QLEN], out)
    return out


def attn_kernel(nd, rows, batch, me, lens, *rest):
    (q_ref, k_ref, v_ref, pre_ref, x_ref, bias_ref, gain_ref) = rest[:7]
    blocks = rest[7 : 7 + nd]
    (p_ref, ctx_ref, mid_ref, n2_ref, w, sems) = rest[7 + nd :]
    step = pl.program_id(0)

    @pl.when(step == 0)
    def _():
        copies = block_copies(me[0], blocks, 3 * rows, rows, w, sems)
        for c in copies:
            c.start()
        for c in copies:
            c.wait()

    lane = lax.broadcasted_iota(jnp.int32, (1, LANES), 1)
    fixed = ((lane >= QLEN) & (lane < QLEN + TOPK)) | (
        (lane >= QLEN + PADK) & (lane < QLEN + PADK + TOPK)
    )
    width = q_ref.shape[1]
    for b in range(batch):
        r = slice(b * QLEN, (b + 1) * QLEN)
        pre = pre_ref[b * PADK : (b + 1) * PADK, :]
        keys = key_list(k_ref[r, :], pre, 0)
        values = key_list(v_ref[r, :], pre, 2)
        valid = fixed | (lane < jnp.minimum(lens[step * batch + b], QLEN))
        for t in range(width // QUAD):
            c = slice(t * QUAD, (t + 1) * QUAD)
            scores = mm_nt(spread_heads(q_ref[r, c]), keys[:, c]) + bias_ref[c, :]
            scores = jnp.where(valid, scores, -1e9)
            e = jnp.exp(scores - jnp.max(scores, axis=1, keepdims=True))
            probs = (e * (1.0 / jnp.sum(e, axis=1, keepdims=True))).astype(BF16)
            p_ref[b, c, :] = probs
            ctx_ref[r, c] = gather_heads(mm(probs, values[:, c])).astype(BF16)
    middle = x_ref[...].astype(F32) + mm(ctx_ref[...], w[...])
    mid_ref[...] = middle
    n2_ref[...] = (middle * rms_factor(middle) * gain_ref[...]).astype(BF16)


def attn_call(me, lens, q, k, v, prefix, x, bias, gain, blocks, rows, batch):
    nd, (count, width) = len(blocks), q.shape
    tile = batch * QLEN
    row_spec = pl.BlockSpec((tile, width), lambda i: (i, 0))
    whole = lambda shape: pl.BlockSpec(shape, lambda i: (0,) * len(shape))
    quest = count // QLEN
    return pl.pallas_call(
        lambda *refs: attn_kernel(nd, rows, batch, *refs),
        grid=(count // tile,),
        in_specs=[SMEM, SMEM, row_spec, row_spec, row_spec]
        + [
            pl.BlockSpec((batch * PADK, prefix.shape[1]), lambda i: (i, 0)),
            row_spec,
            whole(bias.shape),
            whole((1, width)),
        ]
        + [ANY] * nd,
        out_specs=[
            pl.BlockSpec((batch, HEADS * QLEN, LANES), lambda i: (i, 0, 0)),
            row_spec,
            row_spec,
            row_spec,
        ],
        out_shape=[
            jax.ShapeDtypeStruct((quest, HEADS * QLEN, LANES), BF16),
            jax.ShapeDtypeStruct((count, width), BF16),
            jax.ShapeDtypeStruct((count, width), F32),
            jax.ShapeDtypeStruct((count, width), BF16),
        ],
        scratch_shapes=[pltpu.VMEM((width, width), BF16), pltpu.SemaphoreType.DMA((nd,))],
        compiler_params=params(),
        cost_estimate=cost(12 * count * width * width, 0.1, count * width),
        name="attention",
    )(me, lens, q, k, v, prefix, x, bias, gain, *blocks)


def ff_order(nd):
    return list(range(1, nd, 2)) + list(range(0, nd, 2))


def rel_of(step, half):
    return jnp.where(step < half, 2 * step + 1, 2 * (step - half))


def ff_kernel(nd, rows, tile, me, n2_ref, mid_ref, g_ref, gain_ref, *rest):
    half = nd // 2
    in_blocks, back_blocks, sq_blocks = rest[:nd], rest[nd : 2 * nd], rest[2 * nd : 3 * nd]
    (out_ref, gm_ref, gml_ref, dctx_ref, gh_ref, bt_ref) = rest[3 * nd : 3 * nd + 6]
    bm_refs = rest[3 * nd + 6 : 3 * nd + 6 + half]
    (win, wback, wout, act, total, h0, h1, d0, d1, in_sems, back_sems, out_sems) = rest[
        3 * nd + 6 + half :
    ]
    dn2_ref = gm_ref
    step = pl.program_id(0)
    member = me[0]
    count, width = n2_ref.shape
    chunk = wback.shape[1]
    root = math.sqrt(2 / math.pi)
    cube = root * 0.044715

    @pl.when(step == 0)
    def _():
        copies = block_copies(member, in_blocks, 0, rows, win, in_sems)
        for s, k in enumerate(ff_order(nd)):
            copies.append(pltpu.make_async_copy(back_blocks[k], wback.at[s], back_sems.at[s]))
        copies += block_copies(member, sq_blocks, 3 * rows, rows, wout, out_sems)
        for c in copies:
            c.start()
        total[...] = mid_ref[...]
        dn2_ref[...] = jnp.zeros_like(dn2_ref)
        for c in copies:
            c.wait()

    cols = pl.ds(pl.multiple_of((member ^ rel_of(step, half)) * chunk, LANES), chunk)
    w_in = win[:, cols]
    w_back = wback[step]
    hs, ds = (h0, h1), (d0, d1)
    tiles = count // tile
    for m in range(tiles + 1):
        if m < tiles:
            r = slice(m * tile, (m + 1) * tile)
            hs[m % 2][...] = mm(n2_ref[r, :], w_in)
            ds[m % 2][...] = mm_nt(g_ref[r, :], w_back)
        if m > 0:
            r = slice((m - 1) * tile, m * tile)
            h = hs[(m - 1) % 2][...]
            h2 = h * h
            p = 0.5 + 0.5 * jnp.tanh(h * (root + cube * h2))
            a = (h * p).astype(BF16)
            slope = p * (1.0 + (1.0 - p) * (h * (2 * root + 6 * cube * h2)))
            d = (ds[(m - 1) % 2][...] * slope).astype(BF16)
            act[r, :] = a
            gh_ref[0, r, :] = d
            total[r, :] += mm(a, w_back)
            dn2_ref[r, :] += mm_nt(d, w_in)

    @pl.when(step < half)
    def _():
        bt_ref[...] = mm_tn(act[...], g_ref[...]).astype(BF16)[None]

    for kk, bm_ref in enumerate(bm_refs):

        @pl.when(step == half + kk)
        def _():
            bm_ref[...] = mm_tn(act[...], g_ref[...]).astype(BF16)

    @pl.when(step == nd - 1)
    def _():
        for m in range(tiles):
            r = slice(m * tile, (m + 1) * tile)
            out_ref[r, :] = total[r, :].astype(BF16)
            mid, dn2 = mid_ref[r, :], dn2_ref[r, :]
            r2 = rms_factor(mid)
            scaled = dn2 * gain_ref[...]
            gm = (
                g_ref[r, :].astype(F32)
                + r2 * scaled
                - mid * (r2 * r2 * r2 * jnp.mean(scaled * mid, axis=-1, keepdims=True))
            )
            gm_ref[r, :] = gm
            low = gm.astype(BF16)
            gml_ref[r, :] = low
            dctx_ref[r, :] = mm_nt(low, wout[...]).astype(BF16)


def ff_call(me, n2, mid, g, gain, in_blocks, back_blocks, sq_blocks, tile):
    nd, (count, width) = len(in_blocks), n2.shape
    half = nd // 2
    rows, hidden = in_blocks[0].shape
    chunk = back_blocks[0].shape[0]
    once = pl.Buffered(1)
    whole = lambda *shape: pl.BlockSpec(shape, lambda i: (0,) * len(shape))
    held = lambda *shape: pl.BlockSpec(shape, lambda i: (0,) * len(shape), pipeline_mode=once)
    rows_of = lambda dtype: jax.ShapeDtypeStruct((count, width), dtype)
    return pl.pallas_call(
        lambda *refs: ff_kernel(nd, rows, tile, *refs),
        grid=(nd,),
        in_specs=[SMEM] + [held(count, width)] * 3 + [whole(1, width)] + [ANY] * (3 * nd),
        out_specs=[whole(count, width)] * 4
        + [
            pl.BlockSpec((1, count, chunk), lambda i: (i, 0, 0)),
            pl.BlockSpec((1, chunk, width), lambda i: (jnp.minimum(i, half - 1), 0, 0)),
        ]
        + [whole(chunk, width)] * half,
        out_shape=[rows_of(BF16), rows_of(F32), rows_of(BF16), rows_of(BF16)]
        + [
            jax.ShapeDtypeStruct((nd, count, chunk), BF16),
            jax.ShapeDtypeStruct((half, chunk, width), BF16),
        ]
        + [jax.ShapeDtypeStruct((chunk, width), BF16)] * half,
        scratch_shapes=[
            pltpu.VMEM((width, hidden), BF16),
            pltpu.VMEM((nd, chunk, width), BF16),
            pltpu.VMEM((width, width), BF16),
            pltpu.VMEM((count, chunk), BF16),
            pltpu.VMEM((count, width), F32),
        ]
        + [pltpu.VMEM((tile, chunk), F32)] * 4
        + [pltpu.SemaphoreType.DMA((nd,))] * 3,
        compiler_params=params(),
        cost_estimate=cost(10 * count * width * hidden, 1.8, 20 * count * width + 6 * width * hidden),
        name="feed_forward",
    )(me, n2, mid, g, gain, *in_blocks, *back_blocks, *sq_blocks)


def ff_in_kernel(nd, rows, me, n2_ref, gh_ref, it_ref, *rest):
    half = nd // 2
    im_refs, (gin, sems) = rest[:half], rest[half:]
    step = pl.program_id(0)
    width, chunk = gin.shape[1:]
    wide = it_ref.shape[2]

    def copies(at_step):
        at = (me[0] ^ rel_of(at_step, half)) * chunk
        down = pl.ds(pl.multiple_of(at // wide * rows, rows), rows)
        across = pl.ds(pl.multiple_of(at % wide, LANES), chunk)
        out = []
        for kk in range(half):
            for ref, k in ((it_ref.at[kk], 2 * kk + 1), (im_refs[kk], 2 * kk)):
                src = pl.ds(pl.multiple_of((me[0] ^ k) * rows, rows), rows)
                out.append(
                    pltpu.make_async_copy(
                        gin.at[at_step, src], ref.at[down, across], sems.at[at_step, k]
                    )
                )
        return out

    gin[step] = mm_tn(n2_ref[...], gh_ref[0]).astype(BF16)
    for c in copies(step):
        c.start()

    @pl.when(step == nd - 1)
    def _():
        for s in range(nd):
            for c in copies(s):
                c.wait()


def ff_in_call(me, n2, gh, rows):
    (count, width), (nd, _, chunk) = n2.shape, gh.shape
    half = nd // 2
    shape = (rows * nd * chunk // width, width)
    return pl.pallas_call(
        lambda *refs: ff_in_kernel(nd, rows, *refs),
        grid=(nd,),
        in_specs=[
            SMEM,
            pl.BlockSpec((count, width), lambda i: (0, 0)),
            pl.BlockSpec((1, count, chunk), lambda i: (i, 0, 0)),
        ],
        out_specs=[ANY] * (1 + half),
        out_shape=[jax.ShapeDtypeStruct((half,) + shape, BF16)]
        + [jax.ShapeDtypeStruct(shape, BF16)] * half,
        scratch_shapes=[
            pltpu.VMEM((nd, width, chunk), BF16),
            pltpu.SemaphoreType.DMA((nd, nd)),
        ],
        compiler_params=params(),
        cost_estimate=cost(2 * count * width * nd * chunk, 2.0, 2 * nd * chunk * (count + width)),
        name="feed_forward_in",
    )(me, n2, gh)


def attn_back_kernel(batch, *refs):
    (dctx_ref, p_ref, q_ref, k_ref, v_ref, pre_ref, buckets_ref) = refs[:7]
    (dq_ref, dk_ref, dv_ref, dpre_ref, sums_ref, dbias_ref, diagonals) = refs[7:]

    @pl.when(pl.program_id(0) == 0)
    def _():
        dbias_ref[...] = jnp.zeros_like(dbias_ref)

    width = q_ref.shape[1]
    for b in range(batch):
        r = slice(b * QLEN, (b + 1) * QLEN)
        pr = slice(b * PADK, (b + 1) * PADK)
        pre = pre_ref[pr, :]
        keys = key_list(k_ref[r, :], pre, 0)
        values = key_list(v_ref[r, :], pre, 2)
        for t in range(width // QUAD):
            c = slice(t * QUAD, (t + 1) * QUAD)
            gs = spread_heads(dctx_ref[r, c])
            qs = spread_heads(q_ref[r, c])
            low_probs = p_ref[b, c, :]
            probs = low_probs.astype(F32)
            gp = mm_nt(gs, values[:, c])
            dval = mm_tn(low_probs, gs)
            ds = (probs * (gp - jnp.sum(probs * gp, axis=1, keepdims=True))).astype(BF16)
            dbias_ref[c, :] += ds.astype(F32)
            dq_ref[r, c] = gather_heads(mm(ds, keys[:, c])).astype(BF16)
            dkey = mm_tn(ds, qs)
            for ref, first, grad in ((dk_ref, 0, dkey), (dv_ref, 2, dval)):
                low_grad = grad.astype(BF16)
                ref[r, c] = low_grad[:QLEN]
                for s in range(2):
                    at = (first + s) * width + t * QUAD
                    dpre_ref[pr, at : at + QUAD] = low_grad[
                        QLEN + s * PADK : QLEN + (s + 1) * PADK
                    ]

    @pl.when(pl.program_id(0) == pl.num_programs(0) - 1)
    def _():
        token = lax.broadcasted_iota(jnp.int32, (QLEN, LANES), 1) < QLEN
        diagonals[...] = jnp.zeros_like(diagonals)
        places = [lax.broadcasted_iota(jnp.int32, (QLEN, QLEN), axis) for axis in (0, 1)]
        reverse = (places[0] + places[1] == QLEN - 1).astype(F32)
        for h in range(HEADS):
            grads = jnp.where(token, dbias_ref[h * QLEN : (h + 1) * QLEN, :], 0.0)
            grads = jnp.dot(
                reverse, grads, precision=lax.Precision.HIGHEST, preferred_element_type=F32
            )
            grads = pltpu.roll(grads, 0, axis=1, stride=1, stride_axis=0)
            diagonals[h : h + 1, :] = jnp.sum(grads, axis=0, keepdims=True)
        sums_ref[...] = lax.dot_general(
            buckets_ref[...],
            diagonals[...],
            (((1,), (1,)), ((), ())),
            precision=lax.Precision.HIGHEST,
            preferred_element_type=F32,
        )


def attn_back_call(dctx, probs, q, k, v, prefix, batch):
    count, width = q.shape
    tile = batch * QLEN
    row_spec = pl.BlockSpec((tile, width), lambda i: (i, 0))
    pre_spec = pl.BlockSpec((batch * PADK, prefix.shape[1]), lambda i: (i, 0))
    rows_of = jax.ShapeDtypeStruct((count, width), BF16)
    buckets = np.zeros((NB, LANES), np.float32)
    table = bucket_table(QLEN, NB, MAXDIST)
    for offset in range(1 - QLEN, QLEN):
        buckets[:, offset + QLEN - 1] = table[max(0, -offset), max(0, offset)]
    return pl.pallas_call(
        lambda *refs: attn_back_kernel(batch, *refs),
        grid=(count // tile,),
        in_specs=[row_spec, pl.BlockSpec((batch, HEADS * QLEN, LANES), lambda i: (i, 0, 0))]
        + [row_spec] * 3
        + [pre_spec, pl.BlockSpec((NB, LANES), lambda i: (0, 0))],
        out_specs=[row_spec] * 3 + [pre_spec, pl.BlockSpec((NB, LANES), lambda i: (0, 0))],
        out_shape=[rows_of] * 3
        + [
            jax.ShapeDtypeStruct(prefix.shape, BF16),
            jax.ShapeDtypeStruct((NB, LANES), F32),
        ],
        scratch_shapes=[
            pltpu.VMEM((HEADS * QLEN, LANES), F32),
            pltpu.VMEM((LANES, LANES), F32),
        ],
        compiler_params=params(),
        cost_estimate=cost(20 * count * width * width, 1.9, 20 * count * width),
        name="attention_back",
    )(dctx, probs, q, k, v, prefix, jnp.asarray(buckets))


def square_kernel(nd, rows, me, n_ref, ctx_ref, dq_ref, dk_ref, dv_ref, gml_ref, sums, *rest):
    half = nd // 2
    their, mine = rest[0], rest[1 : 1 + half]
    left0, left1, right, full, small, in_sems, out_sems = rest[1 + half :]
    width = right.shape[2]
    loads = [pltpu.make_async_copy(n_ref, left0, in_sems.at[0])]
    for i, ref in enumerate((dq_ref, dk_ref, dv_ref, gml_ref)):
        loads.append(pltpu.make_async_copy(ref, right.at[i], in_sems.at[i + 1]))
    loads.append(pltpu.make_async_copy(ctx_ref, left1, in_sems.at[5]))
    for c in loads:
        c.start()
    stores = []

    def store(kk, k, src, at, size, sem):
        dst = their.at[kk] if k % 2 else mine[kk]
        stores.append(pltpu.make_async_copy(src, dst.at[pl.ds(at, size)], sem))
        stores[-1].start()

    group = sums.shape[0] // nd
    for kk in range(half):
        for k in (2 * kk + 1, 2 * kk):
            small[k] = jnp.zeros(small.shape[1:], BF16)
            at = pl.ds(pl.multiple_of((me[0] ^ k) * group, group), group)
            rows16 = jnp.concatenate(
                [sums[at, :], jnp.zeros((PADK - group, LANES), F32)], axis=0
            )
            small[k, :PADK, :LANES] = rows16.astype(BF16)
            store(kk, k, small.at[k], 4 * rows, EXTRA, out_sems.at[4, k])
    loads[0].wait()
    for i in range(4):
        loads[i + 1].wait()
        if i == 3:
            loads[5].wait()
        left = left1 if i == 3 else left0
        for c in range(0, width, QUAD):
            full[i, c : c + QUAD, :] = mm_tn(left[:, c : c + QUAD], right[i]).astype(BF16)
        for kk in range(half):
            for k in (2 * kk + 1, 2 * kk):
                at = pl.ds(pl.multiple_of((me[0] ^ k) * rows, rows), rows)
                store(kk, k, full.at[i, at], i * rows, rows, out_sems.at[i, k])
    for c in stores:
        c.wait()


def square_call(me, nd, rows, normed, ctx, dq, dk, dv, gml, sums):
    count, width = normed.shape
    half = nd // 2
    size = 4 * rows + EXTRA
    return pl.pallas_call(
        lambda *refs: square_kernel(nd, rows, *refs),
        in_specs=[SMEM] + [ANY] * 6 + [pl.BlockSpec(memory_space=pltpu.VMEM)],
        out_specs=[ANY] * (1 + half),
        out_shape=[jax.ShapeDtypeStruct((half, size, width), BF16)]
        + [jax.ShapeDtypeStruct((size, width), BF16)] * half,
        scratch_shapes=[
            pltpu.VMEM((count, width), BF16),
            pltpu.VMEM((count, width), BF16),
            pltpu.VMEM((4, count, width), BF16),
            pltpu.VMEM((4, width, width), BF16),
            pltpu.VMEM((nd, EXTRA, width), BF16),
            pltpu.SemaphoreType.DMA((6,)),
            pltpu.SemaphoreType.DMA((5, nd)),
        ],
        compiler_params=params(False),
        cost_estimate=cost(8 * count * width * width, 2.0, 12 * count * width + 8 * width * width),
        name="square_grads",
    )(me, normed, ctx, dq, dk, dv, gml, sums)


def input_kernel(nd, rows, me, x_ref, gain_ref, gm_ref, dq_ref, dk_ref, dv_ref, *rest):
    blocks, (gt_ref, w, sems) = rest[:nd], rest[nd:]

    @pl.when(pl.program_id(0) == 0)
    def _():
        copies = []
        for i in range(3):
            copies += block_copies(me[0], blocks, i * rows, rows, w.at[i], sems.at[i])
        for c in copies:
            c.start()
        for c in copies:
            c.wait()

    dn = mm_nt(dq_ref[...], w[0]) + mm_nt(dk_ref[...], w[1]) + mm_nt(dv_ref[...], w[2])
    x = x_ref[...].astype(F32)
    r1 = rms_factor(x)
    scaled = dn * gain_ref[...]
    gt_ref[...] = (
        gm_ref[...]
        + r1 * scaled
        - x * (r1 * r1 * r1 * jnp.mean(scaled * x, axis=-1, keepdims=True))
    )


def input_call(me, x, gain, gm, dq, dk, dv, blocks, rows, tile):
    nd, (count, width) = len(blocks), x.shape
    row_spec = pl.BlockSpec((tile, width), lambda i: (i, 0))
    whole = lambda *shape: pl.BlockSpec(shape, lambda i: (0,) * len(shape))
    return pl.pallas_call(
        lambda *refs: input_kernel(nd, rows, *refs),
        grid=(count // tile,),
        in_specs=[SMEM, row_spec, whole(1, width)] + [row_spec] * 4 + [ANY] * nd,
        out_specs=row_spec,
        out_shape=jax.ShapeDtypeStruct((count, width), F32),
        scratch_shapes=[
            pltpu.VMEM((3, width, width), BF16),
            pltpu.SemaphoreType.DMA((3, nd)),
        ],
        compiler_params=params(),
        cost_estimate=cost(6 * count * width * width, 0.1, 16 * width * width + 6 * width * width),
        name="input_grad",
    )(me, x, gain, gm, dq, dk, dv, *blocks)


def after(value, *earlier):
    return lax.optimization_barrier((value, *earlier))[0]


class Moves:
    def __init__(self, nd, nw):
        self.nd, self.nw = nd, nw
        self.yn = nd // 2
        self.xn = self.yn if nw % self.yn == 0 else 1
        self.zn = nw // self.xn
        self.bits = nw.bit_length() - 1

    def send(self, value, axis, k):
        if axis in ("core", "y"):
            flip = k if axis == "core" else 2 * k
            return lax.ppermute(value, "dp", [(i, i ^ flip) for i in range(self.nd)])
        flip = k if axis == "x" else self.xn * k
        return lax.ppermute(value, "wide", [(i, i ^ flip) for i in range(self.nw)])

    def where(self, axis):
        if axis == "y":
            return lax.axis_index("dp") // 2
        if axis == "x":
            return lax.axis_index("wide") % self.xn
        return lax.axis_index("wide") // self.xn


def by_distance(parts, place):
    parts = list(parts)
    bit = 1
    while bit < len(parts):
        on = (place & bit) != 0
        parts = [jnp.where(on, parts[i ^ bit], parts[i]) for i in range(len(parts))]
        bit *= 2
    return parts


def cut(value, count, axis):
    size = value.shape[axis] // count
    return [lax.slice_in_dim(value, i * size, (i + 1) * size, axis=axis) for i in range(count)]


def summed(values):
    total = values[0].astype(F32)
    for v in values[1:]:
        total = total + v.astype(F32)
    return total


def core_sum(moves, their, mine):
    return mine, moves.send(their, "core", 1)


def by_wide(moves, value):
    *lead, rows, cols = value.shape
    return value.reshape(*lead, moves.nw, rows // moves.nw, cols)


def halves(moves, value, bit):
    *lead, n, r, c = value.shape
    pair = value.reshape(*lead, n // 2, 2, r, c)
    low, high = pair[..., 0, :, :], pair[..., 1, :, :]
    on = ((lax.axis_index("wide") >> bit) & 1) != 0
    return jnp.where(on, high, low), jnp.where(on, low, high)


def send_wide(moves, value, bit):
    return lax.ppermute(value, "wide", [(i, i ^ (1 << bit)) for i in range(moves.nw)])


def gather_dp(moves, shard, y_after=()):
    out = []
    for kk in range(moves.yn):
        out.append(shard if kk == 0 else moves.send(after(shard, *y_after), "y", kk))
    return out


def share_cores(moves, blocks, *deps):
    out = []
    for block in blocks:
        out += [block, moves.send(after(block, *deps), "core", 1)]
    return out


def spread_wide(moves, value):
    r, c = value.shape
    value = value.reshape(1, r, c)
    for bit in reversed(range(moves.bits)):
        got = send_wide(moves, value, bit)
        on = ((lax.axis_index("wide") >> bit) & 1) != 0
        value = jnp.stack([jnp.where(on, got, value), jnp.where(on, value, got)], axis=1)
        value = value.reshape(-1, r, c)
    return value.reshape(-1, c)


def slot_rank(owners):
    same_owner = owners[:, None] == owners[None, :]
    ids = jnp.arange(owners.shape[0])
    return jnp.sum((same_owner & (ids[None, :] < ids[:, None])).astype(jnp.int32), axis=1)


def shards(
    tokens,
    lengths,
    indices,
    memory_table,
    w_query,
    w_key,
    w_value,
    w_out,
    w_in,
    w_back,
    gain_one,
    gain_two,
    rel_bias,
    cotangent,
):
    nd, nw = lax.axis_size("dp"), lax.axis_size("wide")
    moves = Moves(nd, nw)
    dp_index = lax.axis_index("dp")
    me = dp_index.astype(jnp.int32).reshape(1)
    quest = lengths.shape[0]
    count, width = tokens.shape
    rows = w_query.shape[0]
    entries = memory_table.shape[0]
    per_dev = quest * TOPK
    capacity = (per_dev + nw - 1) // nw + 1
    capacity = (capacity + 7) // 8 * 8
    slots = nw * capacity

    flat = indices.reshape(per_dev)
    owner = flat // entries
    rank = slot_rank(owner)
    local = flat - owner * entries
    hit = (owner[None, None, :] == jnp.arange(nw)[:, None, None]) & (
        rank[None, None, :] == jnp.arange(LANES)[None, :, None]
    )
    request = jnp.sum(jnp.where(hit, local[None, None, :] + 1, 0), axis=2) - 1
    hops = [moves.send(lengths.astype(F32), "core", 1)]
    for _ in range(3):
        hops.append(moves.send(hops[-1] + 1.0, "core", 1))
    seen_lengths = (hops[3] - 3.0).astype(jnp.int32)

    packed = pack_call((w_query, w_key, w_value, w_out), gain_one, gain_two, rel_bias)
    asked = lax.all_to_all(after(request, packed), "wide", 0, 0, tiled=True)
    asked = asked[:, :capacity].reshape(slots)
    selection = (asked[:, None] == jnp.arange(entries)[None, :]).astype(BF16)
    outgoing = jnp.dot(selection, memory_table, preferred_element_type=F32).astype(BF16)
    outgoing = outgoing.reshape(nw, capacity, 4 * width)
    incoming = lax.all_to_all(after(outgoing, hops[2]), "wide", 0, 0, tiled=True).reshape(slots, 4 * width)

    square = share_cores(moves, gather_dp(moves, packed, (hops[0],)))

    smalls = jnp.stack([block[4 * rows :] for block in square])
    smalls = jnp.stack(by_distance([smalls[k] for k in range(nd)], dp_index)).astype(F32)
    full_gain_one = smalls[:, 0, :rows].reshape(1, width)
    full_gain_two = smalls[:, 1, :rows].reshape(1, width)
    bias_size = rel_bias.size
    full_bias = smalls[:, 8 : 8 + NB // nd, :HEADS].reshape(NB, HEADS)
    onehot = np.zeros((QLEN, LANES, NB), np.float32)
    onehot[:, :QLEN] = bucket_table(QLEN, NB, MAXDIST)
    onehot = onehot.reshape(QLEN * LANES, NB)
    bias = jnp.dot(
        full_bias.T.astype(BF16), jnp.asarray(onehot.T, BF16), preferred_element_type=F32
    ).reshape(HEADS * QLEN, LANES)

    tile = 4 * QLEN
    q, k, v, normed = qkv_call(me, tokens, full_gain_one, square, rows, tile)
    ins = gather_dp(moves, w_in, (square[2],))
    backs = gather_dp(moves, w_back, (square[2],))

    slot = (owner * capacity + rank).reshape(quest, TOPK)
    slot = jnp.pad(slot, ((0, 0), (0, PADK - TOPK)), constant_values=-1).reshape(quest * PADK)
    slot_hot = (slot[:, None] == jnp.arange(slots)[None, :]).astype(BF16)
    prefix = jnp.dot(
        slot_hot, after(incoming, q, bias), preferred_element_type=F32
    ).astype(BF16)

    probs, ctx, mid, n2 = attn_call(
        me, seen_lengths, q, k, v, prefix, tokens, bias, full_gain_two, square, rows, 4
    )

    ins = share_cores(moves, ins, ctx)
    backs = share_cores(moves, backs, ctx)
    both = jnp.stack([asked, moves.send(after(asked, ctx), "core", 1)])
    far_asked = [moves.send(both, "y", kk) for kk in range(1, moves.yn)]
    rows_asked = jnp.stack([both] + far_asked).reshape(nd * slots)

    layer_out, gm, gml, dctx, gh, back_their, *back_mine = ff_call(
        me, n2, mid, cotangent, full_gain_two, ins, backs, square, tile
    )
    b_terms = core_sum(moves, back_their, back_mine)
    in_their, *in_mine = ff_in_call(me, after(n2, *far_asked), gh, rows)
    b_far = [summed([t[kk] for t in b_terms]).astype(BF16) for kk in range(1, moves.yn)]
    b_near = [moves.send(value, "y", kk + 1) for kk, value in enumerate(b_far)]
    i_terms = core_sum(moves, in_their, jnp.stack(in_mine))
    i_cut = [halves(moves, by_wide(moves, term), 0) for term in i_terms]
    i_keep = [c[0] for c in i_cut]
    i_send = after(summed([c[1] for c in i_cut]).astype(BF16), *b_far)
    i_got = send_wide(moves, i_send, 0)

    dq, dk, dv, dpre, sums = attn_back_call(after(dctx, i_send), probs, q, k, v, prefix, 4)

    b_cut = [
        halves(moves, by_wide(moves, term), 0)
        for term in [t[0] for t in b_terms] + [after(v, dq) for v in b_near]
    ]
    b_keep = [c[0] for c in b_cut]
    b_send = summed([c[1] for c in b_cut]).astype(BF16)
    b_got = send_wide(moves, b_send, 0)
    i_terms = i_keep + [after(i_got, b_send)]
    i_far = [summed([term[kk] for term in i_terms]).astype(BF16) for kk in range(1, moves.yn)]
    i_near = [moves.send(v, "y", kk + 1) for kk, v in enumerate(i_far)]

    returned = mm_tn(slot_hot, after(dpre, b_got, *i_near)).astype(BF16)
    arrived = lax.all_to_all(
        returned.reshape(nw, slots // nw, 4 * width), "wide", 0, 0, tiled=True
    )

    s_their, *s_mine = square_call(
        me, nd, rows, normed, after(ctx, *i_far), dq, dk, dv, gml, sums
    )
    s_terms = core_sum(moves, s_their, s_mine)

    def wide_step(value, bit, *deps):
        keep, send = halves(moves, value, bit)
        got = send_wide(moves, after(send.astype(BF16), *deps), bit)
        return keep + got.astype(F32), got

    p_sum = jnp.stack(
        [summed(b_keep + [after(b_got, s_their)]), summed([term[0] for term in i_terms] + i_near)]
    )
    s_far = [summed([t[kk] for t in s_terms]).astype(BF16) for kk in range(1, moves.yn)]
    s_near = [moves.send(value, "y", kk + 1) for kk, value in enumerate(s_far)]
    p_sum, p_first = wide_step(p_sum, 1, *s_far)

    for bit in range(2, moves.bits):
        p_sum, _ = wide_step(p_sum, bit, arrived)
    p_all = spread_wide(moves, p_sum[:, 0].astype(BF16).reshape(-1, width))
    p_all = p_all.reshape(nw, 2, -1, width)
    grad_back = p_all[:, 0].reshape(w_back.shape).astype(F32)
    grad_in = jnp.concatenate(
        cut(p_all[:, 1].reshape(-1, width), w_in.shape[1] // width, 0), axis=1
    ).astype(F32)

    grad_tokens = input_call(
        me, tokens, full_gain_one, after(gm, *s_far), dq, dk, dv, square, rows, tile
    )
    by_slot = arrived.reshape(slots, nd, 4 * width // nd)
    cols = by_distance([by_slot[:, j] for j in range(nd)], dp_index)
    got = moves.send(jnp.stack(cols[1::2]), "core", 1)
    pairs = [jnp.concatenate([cols[2 * kk], got[kk]], axis=0) for kk in range(moves.yn)]
    pairs_far = [
        moves.send(pairs[kk], "y", kk) for kk in range(1, moves.yn)
    ]
    table_rows = jnp.concatenate([pairs[0]] + pairs_far, axis=0)
    scatter = (jnp.arange(entries)[:, None] == rows_asked[None, :]).astype(BF16)
    grad_table = jnp.dot(scatter, table_rows, preferred_element_type=F32)

    s_sum = by_wide(moves, summed([t[0] for t in s_terms] + s_near))
    s_sum, _ = wide_step(s_sum, 0, grad_tokens, p_first)
    for bit in range(1, moves.bits):
        s_sum, _ = wide_step(s_sum, bit)
    grad_square = spread_wide(moves, s_sum[0].astype(BF16)).astype(F32)

    grad_query, grad_key, grad_value, grad_out = cut(grad_square[: 4 * rows], 4, 0)
    gain_grad = lambda gain, *pairs: sum(
        jnp.sum(weight.astype(F32) * grad, axis=1) for weight, grad in pairs
    ) / gain.astype(F32)
    return (
        layer_out,
        grad_tokens,
        grad_query,
        grad_key,
        grad_value,
        grad_out,
        grad_in,
        grad_back,
        gain_grad(gain_one, (w_query, grad_query), (w_key, grad_key), (w_value, grad_value)),
        gain_grad(gain_two, (w_in, grad_in)),
        grad_square[4 * rows : 4 * rows + NB // nd, :HEADS],
        grad_table,
    )


def solution(mesh):
    split = P(("dp", "wide"), None)
    weight = P("dp", None)
    return jax.shard_map(
        shards,
        mesh=mesh,
        in_specs=(split, P(("dp", "wide")), split, P("wide", None))
        + (weight,) * 6
        + (P("dp"), P("dp"), weight, split),
        out_specs=(split, split) + (weight,) * 6 + (P("dp"), P("dp"), weight, P("wide", "dp")),
        check_vma=False,
    )
```

```python
import math

import jax
import jax.numpy as jnp
import numpy as np
from jax import lax
from jax.experimental import pallas as pl
from jax.experimental.pallas import tpu as pltpu
from jax.sharding import PartitionSpec as P

HEADS = 12
HD = 64
NB = 32
MAXDIST = 128
QLEN = 64
TOPK = 10
PADK = 16
LANES = 128
QUAD = 256
EXTRA = 64
EPS = 1e-06
F32 = jnp.float32
BF16 = jnp.bfloat16
VMEM_BYTES = 58 * 1024 * 1024
ANY = pl.BlockSpec(memory_space=pl.ANY)
SMEM = pl.BlockSpec(memory_space=pltpu.SMEM)


def bucket_table(length, buckets, max_reach):
    half_count = buckets // 2
    near_count = half_count // 2
    onehot = np.zeros((length, length, buckets), np.float32)
    for target in range(length):
        for source in range(length):
            offset = source - target
            bucket = half_count if offset > 0 else 0
            distance = abs(offset)
            if distance < near_count:
                bucket += distance
            else:
                bucket += min(
                    half_count - 1,
                    near_count
                    + int(
                        math.log(distance / near_count)
                        / math.log(max_reach / near_count)
                        * (half_count - near_count)
                    ),
                )
            onehot[target, source, bucket] = 1.0
    return onehot


def mm(a, b):
    return jnp.dot(a, b, preferred_element_type=F32)


def mm_nt(a, b):
    return lax.dot_general(a, b, (((1,), (1,)), ((), ())), preferred_element_type=F32)


def mm_tn(a, b):
    return lax.dot_general(a, b, (((0,), (0,)), ((), ())), preferred_element_type=F32)


def cost(flops, scale, size):
    return pl.CostEstimate(flops=int(scale * flops), bytes_accessed=int(size), transcendentals=0)


def params(grid=True):
    return pltpu.CompilerParams(
        vmem_limit_bytes=VMEM_BYTES,
        **(dict(dimension_semantics=("arbitrary",)) if grid else {}),
    )


def rms_factor(values):
    return lax.rsqrt(jnp.mean(values * values, axis=-1, keepdims=True) + EPS)


def block_copies(member, blocks, first, rows, target, sems):
    return [
        pltpu.make_async_copy(
            block.at[pl.ds(first, rows)],
            target.at[pl.ds(pl.multiple_of((member ^ k) * rows, rows), rows)],
            sems.at[k],
        )
        for k, block in enumerate(blocks)
    ]


def pack_kernel(*refs):
    (q_ref, k_ref, v_ref, o_ref, gains_ref, bias_ref, out_ref, small) = refs
    rows = q_ref.shape[0]
    for i, ref in enumerate((q_ref, k_ref, v_ref, o_ref)):
        out_ref[i * rows : (i + 1) * rows, :] = ref[...]
    small[...] = jnp.zeros_like(small)
    small[0:2, :rows] = gains_ref[...].astype(F32)
    small[8 : 8 + bias_ref.shape[0], : bias_ref.shape[1]] = bias_ref[...].astype(F32)
    out_ref[4 * rows :, :] = small[...].astype(BF16)


def pack_call(squares, gain_one, gain_two, rel_bias):
    rows, width = squares[0].shape
    vmem = pl.BlockSpec(memory_space=pltpu.VMEM)
    return pl.pallas_call(
        pack_kernel,
        in_specs=[vmem] * 6,
        out_specs=vmem,
        out_shape=jax.ShapeDtypeStruct((4 * rows + PADK, width), BF16),
        scratch_shapes=[pltpu.VMEM((PADK, width), F32)],
        compiler_params=params(False),
        cost_estimate=cost(0, 1, 16 * rows * width),
        name="pack",
    )(*squares, jnp.stack([gain_one, gain_two]), rel_bias)


def qkv_kernel(nd, rows, me, x_ref, gain_ref, *rest):
    blocks, (q_ref, k_ref, v_ref, n_ref, w, sems) = rest[:nd], rest[nd:]

    @pl.when(pl.program_id(0) == 0)
    def _():
        copies = []
        for i in range(3):
            copies += block_copies(me[0], blocks, i * rows, rows, w.at[i], sems.at[i])
        for c in copies:
            c.start()
        for c in copies:
            c.wait()

    x = x_ref[...].astype(F32)
    normed = (x * rms_factor(x) * gain_ref[...]).astype(BF16)
    n_ref[...] = normed
    for i, out in enumerate((q_ref, k_ref, v_ref)):
        out[...] = mm(normed, w[i]).astype(BF16)


def qkv_call(me, x, gain, blocks, rows, tile):
    nd, (count, width) = len(blocks), x.shape
    row_spec = pl.BlockSpec((tile, width), lambda i: (i, 0))
    return pl.pallas_call(
        lambda *refs: qkv_kernel(nd, rows, *refs),
        grid=(count // tile,),
        in_specs=[SMEM, row_spec, pl.BlockSpec((1, width), lambda i: (0, 0))] + [ANY] * nd,
        out_specs=[row_spec] * 4,
        out_shape=[jax.ShapeDtypeStruct((count, width), BF16)] * 4,
        scratch_shapes=[
            pltpu.VMEM((3, width, width), BF16),
            pltpu.SemaphoreType.DMA((3, nd)),
        ],
        compiler_params=params(),
        cost_estimate=cost(6 * count * width * width, 0.1, count * width + 6 * width * width),
        name="norm_qkv",
    )(me, x, gain, *blocks)


def key_list(tok, pre, first):
    width = tok.shape[1]
    return jnp.concatenate(
        [
            tok,
            pre[:, first * width : (first + 1) * width],
            pre[:, (first + 1) * width : (first + 2) * width],
            jnp.zeros((LANES - QLEN - 2 * PADK, width), tok.dtype),
        ],
        axis=0,
    )


def spread_heads(part):
    head = lax.broadcasted_iota(jnp.int32, part.shape, 1) // HD
    return jnp.concatenate(
        [jnp.where(head == h, part, jnp.zeros_like(part)) for h in range(QUAD // HD)], axis=0
    )


def gather_heads(full):
    head = lax.broadcasted_iota(jnp.int32, (QLEN, QUAD), 1) // HD
    out = full[:QLEN]
    for h in range(1, QUAD // HD):
        out = jnp.where(head == h, full[h * QLEN : (h + 1) * QLEN], out)
    return out


def attn_kernel(nd, rows, batch, me, lens, *rest):
    (q_ref, k_ref, v_ref, pre_ref, x_ref, bias_ref, gain_ref) = rest[:7]
    blocks = rest[7 : 7 + nd]
    (p_ref, ctx_ref, mid_ref, n2_ref, w, sems) = rest[7 + nd :]
    step = pl.program_id(0)

    @pl.when(step == 0)
    def _():
        copies = block_copies(me[0], blocks, 3 * rows, rows, w, sems)
        for c in copies:
            c.start()
        for c in copies:
            c.wait()

    lane = lax.broadcasted_iota(jnp.int32, (1, LANES), 1)
    fixed = ((lane >= QLEN) & (lane < QLEN + TOPK)) | (
        (lane >= QLEN + PADK) & (lane < QLEN + PADK + TOPK)
    )
    width = q_ref.shape[1]
    for b in range(batch):
        r = slice(b * QLEN, (b + 1) * QLEN)
        pre = pre_ref[b * PADK : (b + 1) * PADK, :]
        keys = key_list(k_ref[r, :], pre, 0)
        values = key_list(v_ref[r, :], pre, 2)
        valid = fixed | (lane < jnp.minimum(lens[step * batch + b], QLEN))
        for t in range(width // QUAD):
            c = slice(t * QUAD, (t + 1) * QUAD)
            scores = mm_nt(spread_heads(q_ref[r, c]), keys[:, c]) + bias_ref[c, :]
            scores = jnp.where(valid, scores, -1e9)
            e = jnp.exp(scores - jnp.max(scores, axis=1, keepdims=True))
            probs = (e * (1.0 / jnp.sum(e, axis=1, keepdims=True))).astype(BF16)
            p_ref[b, c, :] = probs
            ctx_ref[r, c] = gather_heads(mm(probs, values[:, c])).astype(BF16)
    middle = x_ref[...].astype(F32) + mm(ctx_ref[...], w[...])
    mid_ref[...] = middle
    n2_ref[...] = (middle * rms_factor(middle) * gain_ref[...]).astype(BF16)


def attn_call(me, lens, q, k, v, prefix, x, bias, gain, blocks, rows, batch):
    nd, (count, width) = len(blocks), q.shape
    tile = batch * QLEN
    row_spec = pl.BlockSpec((tile, width), lambda i: (i, 0))
    whole = lambda shape: pl.BlockSpec(shape, lambda i: (0,) * len(shape))
    quest = count // QLEN
    return pl.pallas_call(
        lambda *refs: attn_kernel(nd, rows, batch, *refs),
        grid=(count // tile,),
        in_specs=[SMEM, SMEM, row_spec, row_spec, row_spec]
        + [
            pl.BlockSpec((batch * PADK, prefix.shape[1]), lambda i: (i, 0)),
            row_spec,
            whole(bias.shape),
            whole((1, width)),
        ]
        + [ANY] * nd,
        out_specs=[
            pl.BlockSpec((batch, HEADS * QLEN, LANES), lambda i: (i, 0, 0)),
            row_spec,
            row_spec,
            row_spec,
        ],
        out_shape=[
            jax.ShapeDtypeStruct((quest, HEADS * QLEN, LANES), BF16),
            jax.ShapeDtypeStruct((count, width), BF16),
            jax.ShapeDtypeStruct((count, width), F32),
            jax.ShapeDtypeStruct((count, width), BF16),
        ],
        scratch_shapes=[pltpu.VMEM((width, width), BF16), pltpu.SemaphoreType.DMA((nd,))],
        compiler_params=params(),
        cost_estimate=cost(12 * count * width * width, 0.1, count * width),
        name="attention",
    )(me, lens, q, k, v, prefix, x, bias, gain, *blocks)


def ff_order(nd):
    return list(range(1, nd, 2)) + list(range(0, nd, 2))


def rel_of(step, half):
    return jnp.where(step < half, 2 * step + 1, 2 * (step - half))


def ff_kernel(nd, rows, tile, me, n2_ref, mid_ref, g_ref, gain_ref, *rest):
    half = nd // 2
    in_blocks, back_blocks, sq_blocks = rest[:nd], rest[nd : 2 * nd], rest[2 * nd : 3 * nd]
    (out_ref, gm_ref, gml_ref, dctx_ref, gh_ref, bt_ref) = rest[3 * nd : 3 * nd + 6]
    bm_refs = rest[3 * nd + 6 : 3 * nd + 6 + half]
    (win, wback, wout, act, total, h0, h1, d0, d1, in_sems, back_sems, out_sems) = rest[
        3 * nd + 6 + half :
    ]
    dn2_ref = gm_ref
    step = pl.program_id(0)
    member = me[0]
    count, width = n2_ref.shape
    chunk = wback.shape[1]
    root = math.sqrt(2 / math.pi)
    cube = root * 0.044715

    @pl.when(step == 0)
    def _():
        copies = block_copies(member, in_blocks, 0, rows, win, in_sems)
        for s, k in enumerate(ff_order(nd)):
            copies.append(pltpu.make_async_copy(back_blocks[k], wback.at[s], back_sems.at[s]))
        copies += block_copies(member, sq_blocks, 3 * rows, rows, wout, out_sems)
        for c in copies:
            c.start()
        total[...] = mid_ref[...]
        dn2_ref[...] = jnp.zeros_like(dn2_ref)
        for c in copies:
            c.wait()

    cols = pl.ds(pl.multiple_of((member ^ rel_of(step, half)) * chunk, LANES), chunk)
    w_in = win[:, cols]
    w_back = wback[step]
    hs, ds = (h0, h1), (d0, d1)
    tiles = count // tile
    for m in range(tiles + 1):
        if m < tiles:
            r = slice(m * tile, (m + 1) * tile)
            hs[m % 2][...] = mm(n2_ref[r, :], w_in)
            ds[m % 2][...] = mm_nt(g_ref[r, :], w_back)
        if m > 0:
            r = slice((m - 1) * tile, m * tile)
            h = hs[(m - 1) % 2][...]
            h2 = h * h
            p = 0.5 + 0.5 * jnp.tanh(h * (root + cube * h2))
            a = (h * p).astype(BF16)
            slope = p * (1.0 + (1.0 - p) * (h * (2 * root + 6 * cube * h2)))
            d = (ds[(m - 1) % 2][...] * slope).astype(BF16)
            act[r, :] = a
            gh_ref[0, r, :] = d
            total[r, :] += mm(a, w_back)
            dn2_ref[r, :] += mm_nt(d, w_in)

    @pl.when(step < half)
    def _():
        bt_ref[...] = mm_tn(act[...], g_ref[...]).astype(BF16)[None]

    for kk, bm_ref in enumerate(bm_refs):

        @pl.when(step == half + kk)
        def _():
            bm_ref[...] = mm_tn(act[...], g_ref[...]).astype(BF16)

    @pl.when(step == nd - 1)
    def _():
        for m in range(tiles):
            r = slice(m * tile, (m + 1) * tile)
            out_ref[r, :] = total[r, :].astype(BF16)
            mid, dn2 = mid_ref[r, :], dn2_ref[r, :]
            r2 = rms_factor(mid)
            scaled = dn2 * gain_ref[...]
            gm = (
                g_ref[r, :].astype(F32)
                + r2 * scaled
                - mid * (r2 * r2 * r2 * jnp.mean(scaled * mid, axis=-1, keepdims=True))
            )
            gm_ref[r, :] = gm
            low = gm.astype(BF16)
            gml_ref[r, :] = low
            dctx_ref[r, :] = mm_nt(low, wout[...]).astype(BF16)


def ff_call(me, n2, mid, g, gain, in_blocks, back_blocks, sq_blocks, tile):
    nd, (count, width) = len(in_blocks), n2.shape
    half = nd // 2
    rows, hidden = in_blocks[0].shape
    chunk = back_blocks[0].shape[0]
    once = pl.Buffered(1)
    whole = lambda *shape: pl.BlockSpec(shape, lambda i: (0,) * len(shape))
    held = lambda *shape: pl.BlockSpec(shape, lambda i: (0,) * len(shape), pipeline_mode=once)
    rows_of = lambda dtype: jax.ShapeDtypeStruct((count, width), dtype)
    return pl.pallas_call(
        lambda *refs: ff_kernel(nd, rows, tile, *refs),
        grid=(nd,),
        in_specs=[SMEM] + [held(count, width)] * 3 + [whole(1, width)] + [ANY] * (3 * nd),
        out_specs=[whole(count, width)] * 4
        + [
            pl.BlockSpec((1, count, chunk), lambda i: (i, 0, 0)),
            pl.BlockSpec((1, chunk, width), lambda i: (jnp.minimum(i, half - 1), 0, 0)),
        ]
        + [whole(chunk, width)] * half,
        out_shape=[rows_of(BF16), rows_of(F32), rows_of(BF16), rows_of(BF16)]
        + [
            jax.ShapeDtypeStruct((nd, count, chunk), BF16),
            jax.ShapeDtypeStruct((half, chunk, width), BF16),
        ]
        + [jax.ShapeDtypeStruct((chunk, width), BF16)] * half,
        scratch_shapes=[
            pltpu.VMEM((width, hidden), BF16),
            pltpu.VMEM((nd, chunk, width), BF16),
            pltpu.VMEM((width, width), BF16),
            pltpu.VMEM((count, chunk), BF16),
            pltpu.VMEM((count, width), F32),
        ]
        + [pltpu.VMEM((tile, chunk), F32)] * 4
        + [pltpu.SemaphoreType.DMA((nd,))] * 3,
        compiler_params=params(),
        cost_estimate=cost(10 * count * width * hidden, 1.8, 20 * count * width + 6 * width * hidden),
        name="feed_forward",
    )(me, n2, mid, g, gain, *in_blocks, *back_blocks, *sq_blocks)


def ff_in_kernel(nd, rows, me, n2_ref, gh_ref, it_ref, *rest):
    half = nd // 2
    im_refs, (gin, sems) = rest[:half], rest[half:]
    step = pl.program_id(0)
    width, chunk = gin.shape[1:]
    wide = it_ref.shape[2]

    def copies(at_step):
        at = (me[0] ^ rel_of(at_step, half)) * chunk
        down = pl.ds(pl.multiple_of(at // wide * rows, rows), rows)
        across = pl.ds(pl.multiple_of(at % wide, LANES), chunk)
        out = []
        for kk in range(half):
            for ref, k in ((it_ref.at[kk], 2 * kk + 1), (im_refs[kk], 2 * kk)):
                src = pl.ds(pl.multiple_of((me[0] ^ k) * rows, rows), rows)
                out.append(
                    pltpu.make_async_copy(
                        gin.at[at_step, src], ref.at[down, across], sems.at[at_step, k]
                    )
                )
        return out

    gin[step] = mm_tn(n2_ref[...], gh_ref[0]).astype(BF16)
    for c in copies(step):
        c.start()

    @pl.when(step == nd - 1)
    def _():
        for s in range(nd):
            for c in copies(s):
                c.wait()


def ff_in_call(me, n2, gh, rows):
    (count, width), (nd, _, chunk) = n2.shape, gh.shape
    half = nd // 2
    shape = (rows * nd * chunk // width, width)
    return pl.pallas_call(
        lambda *refs: ff_in_kernel(nd, rows, *refs),
        grid=(nd,),
        in_specs=[
            SMEM,
            pl.BlockSpec((count, width), lambda i: (0, 0)),
            pl.BlockSpec((1, count, chunk), lambda i: (i, 0, 0)),
        ],
        out_specs=[ANY] * (1 + half),
        out_shape=[jax.ShapeDtypeStruct((half,) + shape, BF16)]
        + [jax.ShapeDtypeStruct(shape, BF16)] * half,
        scratch_shapes=[
            pltpu.VMEM((nd, width, chunk), BF16),
            pltpu.SemaphoreType.DMA((nd, nd)),
        ],
        compiler_params=params(),
        cost_estimate=cost(2 * count * width * nd * chunk, 2.0, 2 * nd * chunk * (count + width)),
        name="feed_forward_in",
    )(me, n2, gh)


def attn_back_kernel(batch, *refs):
    (dctx_ref, p_ref, q_ref, k_ref, v_ref, pre_ref, buckets_ref) = refs[:7]
    (dq_ref, dk_ref, dv_ref, dpre_ref, sums_ref, dbias_ref, diagonals) = refs[7:]

    @pl.when(pl.program_id(0) == 0)
    def _():
        dbias_ref[...] = jnp.zeros_like(dbias_ref)

    width = q_ref.shape[1]
    for b in range(batch):
        r = slice(b * QLEN, (b + 1) * QLEN)
        pr = slice(b * PADK, (b + 1) * PADK)
        pre = pre_ref[pr, :]
        keys = key_list(k_ref[r, :], pre, 0)
        values = key_list(v_ref[r, :], pre, 2)
        for t in range(width // QUAD):
            c = slice(t * QUAD, (t + 1) * QUAD)
            gs = spread_heads(dctx_ref[r, c])
            qs = spread_heads(q_ref[r, c])
            low_probs = p_ref[b, c, :]
            probs = low_probs.astype(F32)
            gp = mm_nt(gs, values[:, c])
            dval = mm_tn(low_probs, gs)
            ds = (probs * (gp - jnp.sum(probs * gp, axis=1, keepdims=True))).astype(BF16)
            dbias_ref[c, :] += ds.astype(F32)
            dq_ref[r, c] = gather_heads(mm(ds, keys[:, c])).astype(BF16)
            dkey = mm_tn(ds, qs)
            for ref, first, grad in ((dk_ref, 0, dkey), (dv_ref, 2, dval)):
                low_grad = grad.astype(BF16)
                ref[r, c] = low_grad[:QLEN]
                for s in range(2):
                    at = (first + s) * width + t * QUAD
                    dpre_ref[pr, at : at + QUAD] = low_grad[
                        QLEN + s * PADK : QLEN + (s + 1) * PADK
                    ]

    @pl.when(pl.program_id(0) == pl.num_programs(0) - 1)
    def _():
        token = lax.broadcasted_iota(jnp.int32, (QLEN, LANES), 1) < QLEN
        diagonals[...] = jnp.zeros_like(diagonals)
        places = [lax.broadcasted_iota(jnp.int32, (QLEN, QLEN), axis) for axis in (0, 1)]
        reverse = (places[0] + places[1] == QLEN - 1).astype(F32)
        for h in range(HEADS):
            grads = jnp.where(token, dbias_ref[h * QLEN : (h + 1) * QLEN, :], 0.0)
            grads = jnp.dot(
                reverse, grads, precision=lax.Precision.HIGHEST, preferred_element_type=F32
            )
            grads = pltpu.roll(grads, 0, axis=1, stride=1, stride_axis=0)
            diagonals[h : h + 1, :] = jnp.sum(grads, axis=0, keepdims=True)
        sums_ref[...] = lax.dot_general(
            buckets_ref[...],
            diagonals[...],
            (((1,), (1,)), ((), ())),
            precision=lax.Precision.HIGHEST,
            preferred_element_type=F32,
        )


def attn_back_call(dctx, probs, q, k, v, prefix, batch):
    count, width = q.shape
    tile = batch * QLEN
    row_spec = pl.BlockSpec((tile, width), lambda i: (i, 0))
    pre_spec = pl.BlockSpec((batch * PADK, prefix.shape[1]), lambda i: (i, 0))
    rows_of = jax.ShapeDtypeStruct((count, width), BF16)
    buckets = np.zeros((NB, LANES), np.float32)
    table = bucket_table(QLEN, NB, MAXDIST)
    for offset in range(1 - QLEN, QLEN):
        buckets[:, offset + QLEN - 1] = table[max(0, -offset), max(0, offset)]
    return pl.pallas_call(
        lambda *refs: attn_back_kernel(batch, *refs),
        grid=(count // tile,),
        in_specs=[row_spec, pl.BlockSpec((batch, HEADS * QLEN, LANES), lambda i: (i, 0, 0))]
        + [row_spec] * 3
        + [pre_spec, pl.BlockSpec((NB, LANES), lambda i: (0, 0))],
        out_specs=[row_spec] * 3 + [pre_spec, pl.BlockSpec((NB, LANES), lambda i: (0, 0))],
        out_shape=[rows_of] * 3
        + [
            jax.ShapeDtypeStruct(prefix.shape, BF16),
            jax.ShapeDtypeStruct((NB, LANES), F32),
        ],
        scratch_shapes=[
            pltpu.VMEM((HEADS * QLEN, LANES), F32),
            pltpu.VMEM((LANES, LANES), F32),
        ],
        compiler_params=params(),
        cost_estimate=cost(20 * count * width * width, 1.9, 20 * count * width),
        name="attention_back",
    )(dctx, probs, q, k, v, prefix, jnp.asarray(buckets))


def square_kernel(nd, rows, me, n_ref, ctx_ref, dq_ref, dk_ref, dv_ref, gml_ref, sums, *rest):
    half = nd // 2
    their, mine = rest[0], rest[1 : 1 + half]
    left0, left1, right, full, small, in_sems, out_sems = rest[1 + half :]
    width = right.shape[2]
    loads = [pltpu.make_async_copy(n_ref, left0, in_sems.at[0])]
    for i, ref in enumerate((dq_ref, dk_ref, dv_ref, gml_ref)):
        loads.append(pltpu.make_async_copy(ref, right.at[i], in_sems.at[i + 1]))
    loads.append(pltpu.make_async_copy(ctx_ref, left1, in_sems.at[5]))
    for c in loads:
        c.start()
    stores = []

    def store(kk, k, src, at, size, sem):
        dst = their.at[kk] if k % 2 else mine[kk]
        stores.append(pltpu.make_async_copy(src, dst.at[pl.ds(at, size)], sem))
        stores[-1].start()

    group = sums.shape[0] // nd
    for kk in range(half):
        for k in (2 * kk + 1, 2 * kk):
            small[k] = jnp.zeros(small.shape[1:], BF16)
            at = pl.ds(pl.multiple_of((me[0] ^ k) * group, group), group)
            rows16 = jnp.concatenate(
                [sums[at, :], jnp.zeros((PADK - group, LANES), F32)], axis=0
            )
            small[k, :PADK, :LANES] = rows16.astype(BF16)
            store(kk, k, small.at[k], 4 * rows, EXTRA, out_sems.at[4, k])
    loads[0].wait()
    for i in range(4):
        loads[i + 1].wait()
        if i == 3:
            loads[5].wait()
        left = left1 if i == 3 else left0
        for c in range(0, width, QUAD):
            full[i, c : c + QUAD, :] = mm_tn(left[:, c : c + QUAD], right[i]).astype(BF16)
        for kk in range(half):
            for k in (2 * kk + 1, 2 * kk):
                at = pl.ds(pl.multiple_of((me[0] ^ k) * rows, rows), rows)
                store(kk, k, full.at[i, at], i * rows, rows, out_sems.at[i, k])
    for c in stores:
        c.wait()


def square_call(me, nd, rows, normed, ctx, dq, dk, dv, gml, sums):
    count, width = normed.shape
    half = nd // 2
    size = 4 * rows + EXTRA
    return pl.pallas_call(
        lambda *refs: square_kernel(nd, rows, *refs),
        in_specs=[SMEM] + [ANY] * 6 + [pl.BlockSpec(memory_space=pltpu.VMEM)],
        out_specs=[ANY] * (1 + half),
        out_shape=[jax.ShapeDtypeStruct((half, size, width), BF16)]
        + [jax.ShapeDtypeStruct((size, width), BF16)] * half,
        scratch_shapes=[
            pltpu.VMEM((count, width), BF16),
            pltpu.VMEM((count, width), BF16),
            pltpu.VMEM((4, count, width), BF16),
            pltpu.VMEM((4, width, width), BF16),
            pltpu.VMEM((nd, EXTRA, width), BF16),
            pltpu.SemaphoreType.DMA((6,)),
            pltpu.SemaphoreType.DMA((5, nd)),
        ],
        compiler_params=params(False),
        cost_estimate=cost(8 * count * width * width, 2.0, 12 * count * width + 8 * width * width),
        name="square_grads",
    )(me, normed, ctx, dq, dk, dv, gml, sums)


def input_kernel(nd, rows, me, x_ref, gain_ref, gm_ref, dq_ref, dk_ref, dv_ref, *rest):
    blocks, (gt_ref, w, sems) = rest[:nd], rest[nd:]

    @pl.when(pl.program_id(0) == 0)
    def _():
        copies = []
        for i in range(3):
            copies += block_copies(me[0], blocks, i * rows, rows, w.at[i], sems.at[i])
        for c in copies:
            c.start()
        for c in copies:
            c.wait()

    dn = mm_nt(dq_ref[...], w[0]) + mm_nt(dk_ref[...], w[1]) + mm_nt(dv_ref[...], w[2])
    x = x_ref[...].astype(F32)
    r1 = rms_factor(x)
    scaled = dn * gain_ref[...]
    gt_ref[...] = (
        gm_ref[...]
        + r1 * scaled
        - x * (r1 * r1 * r1 * jnp.mean(scaled * x, axis=-1, keepdims=True))
    )


def input_call(me, x, gain, gm, dq, dk, dv, blocks, rows, tile):
    nd, (count, width) = len(blocks), x.shape
    row_spec = pl.BlockSpec((tile, width), lambda i: (i, 0))
    whole = lambda *shape: pl.BlockSpec(shape, lambda i: (0,) * len(shape))
    return pl.pallas_call(
        lambda *refs: input_kernel(nd, rows, *refs),
        grid=(count // tile,),
        in_specs=[SMEM, row_spec, whole(1, width)] + [row_spec] * 4 + [ANY] * nd,
        out_specs=row_spec,
        out_shape=jax.ShapeDtypeStruct((count, width), F32),
        scratch_shapes=[
            pltpu.VMEM((3, width, width), BF16),
            pltpu.SemaphoreType.DMA((3, nd)),
        ],
        compiler_params=params(),
        cost_estimate=cost(6 * count * width * width, 0.1, 16 * width * width + 6 * width * width),
        name="input_grad",
    )(me, x, gain, gm, dq, dk, dv, *blocks)


def after(value, *earlier):
    return lax.optimization_barrier((value, *earlier))[0]


class Moves:
    def __init__(self, nd, nw):
        self.nd, self.nw = nd, nw
        self.yn = nd // 2
        self.xn = self.yn if nw % self.yn == 0 else 1
        self.zn = nw // self.xn
        self.bits = nw.bit_length() - 1

    def send(self, value, axis, k):
        if axis in ("core", "y"):
            flip = k if axis == "core" else 2 * k
            return lax.ppermute(value, "dp", [(i, i ^ flip) for i in range(self.nd)])
        flip = k if axis == "x" else self.xn * k
        return lax.ppermute(value, "wide", [(i, i ^ flip) for i in range(self.nw)])

    def where(self, axis):
        if axis == "y":
            return lax.axis_index("dp") // 2
        if axis == "x":
            return lax.axis_index("wide") % self.xn
        return lax.axis_index("wide") // self.xn


def by_distance(parts, place):
    parts = list(parts)
    bit = 1
    while bit < len(parts):
        on = (place & bit) != 0
        parts = [jnp.where(on, parts[i ^ bit], parts[i]) for i in range(len(parts))]
        bit *= 2
    return parts


def cut(value, count, axis):
    size = value.shape[axis] // count
    return [lax.slice_in_dim(value, i * size, (i + 1) * size, axis=axis) for i in range(count)]


def summed(values):
    total = values[0].astype(F32)
    for v in values[1:]:
        total = total + v.astype(F32)
    return total


def core_sum(moves, their, mine):
    return mine, moves.send(their, "core", 1)


def by_wide(moves, value):
    *lead, rows, cols = value.shape
    return value.reshape(*lead, moves.nw, rows // moves.nw, cols)


def halves(moves, value, bit):
    *lead, n, r, c = value.shape
    pair = value.reshape(*lead, n // 2, 2, r, c)
    low, high = pair[..., 0, :, :], pair[..., 1, :, :]
    on = ((lax.axis_index("wide") >> bit) & 1) != 0
    return jnp.where(on, high, low), jnp.where(on, low, high)


def send_wide(moves, value, bit):
    return lax.ppermute(value, "wide", [(i, i ^ (1 << bit)) for i in range(moves.nw)])


def gather_dp(moves, shard, y_after=()):
    out = []
    for kk in range(moves.yn):
        out.append(shard if kk == 0 else moves.send(after(shard, *y_after), "y", kk))
    return out


def share_cores(moves, blocks, *deps):
    out = []
    for i, block in enumerate(blocks):
        out += [block, moves.send(after(block, *deps) if i else block, "core", 1)]
    return out


def spread_wide(moves, value):
    r, c = value.shape
    value = value.reshape(1, r, c)
    for bit in reversed(range(moves.bits)):
        got = send_wide(moves, value, bit)
        on = ((lax.axis_index("wide") >> bit) & 1) != 0
        value = jnp.stack([jnp.where(on, got, value), jnp.where(on, value, got)], axis=1)
        value = value.reshape(-1, r, c)
    return value.reshape(-1, c)


def slot_rank(owners):
    same_owner = owners[:, None] == owners[None, :]
    ids = jnp.arange(owners.shape[0])
    return jnp.sum((same_owner & (ids[None, :] < ids[:, None])).astype(jnp.int32), axis=1)


def shards(
    tokens,
    lengths,
    indices,
    memory_table,
    w_query,
    w_key,
    w_value,
    w_out,
    w_in,
    w_back,
    gain_one,
    gain_two,
    rel_bias,
    cotangent,
):
    nd, nw = lax.axis_size("dp"), lax.axis_size("wide")
    moves = Moves(nd, nw)
    dp_index = lax.axis_index("dp")
    me = dp_index.astype(jnp.int32).reshape(1)
    quest = lengths.shape[0]
    count, width = tokens.shape
    rows = w_query.shape[0]
    entries = memory_table.shape[0]
    per_dev = quest * TOPK
    capacity = (per_dev + nw - 1) // nw + 1
    capacity = (capacity + 7) // 8 * 8
    slots = nw * capacity

    flat = indices.reshape(per_dev)
    owner = flat // entries
    rank = slot_rank(owner)
    local = flat - owner * entries
    hit = (owner[None, None, :] == jnp.arange(nw)[:, None, None]) & (
        rank[None, None, :] == jnp.arange(LANES)[None, :, None]
    )
    request = jnp.sum(jnp.where(hit, local[None, None, :] + 1, 0), axis=2) - 1
    hops = [moves.send(lengths.astype(F32), "core", 1)]
    for _ in range(3):
        hops.append(moves.send(hops[-1] + 1.0, "core", 1))
    seen_lengths = (hops[3] - 3.0).astype(jnp.int32)

    packed = pack_call((w_query, w_key, w_value, w_out), gain_one, gain_two, rel_bias)
    asked = lax.all_to_all(after(request, packed), "wide", 0, 0, tiled=True)
    asked = asked[:, :capacity].reshape(slots)
    selection = (asked[:, None] == jnp.arange(entries)[None, :]).astype(BF16)
    outgoing = jnp.dot(selection, memory_table, preferred_element_type=F32).astype(BF16)
    outgoing = outgoing.reshape(nw, capacity, 4 * width)
    incoming = lax.all_to_all(after(outgoing, hops[2]), "wide", 0, 0, tiled=True).reshape(slots, 4 * width)

    square = share_cores(moves, gather_dp(moves, packed, (hops[0],)))

    smalls = jnp.stack([block[4 * rows :] for block in square])
    smalls = jnp.stack(by_distance([smalls[k] for k in range(nd)], dp_index)).astype(F32)
    full_gain_one = smalls[:, 0, :rows].reshape(1, width)
    full_gain_two = smalls[:, 1, :rows].reshape(1, width)
    bias_size = rel_bias.size
    full_bias = smalls[:, 8 : 8 + NB // nd, :HEADS].reshape(NB, HEADS)
    onehot = np.zeros((QLEN, LANES, NB), np.float32)
    onehot[:, :QLEN] = bucket_table(QLEN, NB, MAXDIST)
    onehot = onehot.reshape(QLEN * LANES, NB)
    bias = jnp.dot(
        full_bias.T.astype(BF16), jnp.asarray(onehot.T, BF16), preferred_element_type=F32
    ).reshape(HEADS * QLEN, LANES)

    tile = 4 * QLEN
    q, k, v, normed = qkv_call(me, tokens, full_gain_one, square, rows, tile)
    ins = gather_dp(moves, w_in, (square[2],))
    backs = gather_dp(moves, w_back, (square[2],))

    slot = (owner * capacity + rank).reshape(quest, TOPK)
    slot = jnp.pad(slot, ((0, 0), (0, PADK - TOPK)), constant_values=-1).reshape(quest * PADK)
    slot_hot = (slot[:, None] == jnp.arange(slots)[None, :]).astype(BF16)
    prefix = jnp.dot(
        slot_hot, after(incoming, q, bias), preferred_element_type=F32
    ).astype(BF16)

    probs, ctx, mid, n2 = attn_call(
        me, seen_lengths, q, k, v, prefix, tokens, bias, full_gain_two, square, rows, 4
    )

    ins = share_cores(moves, ins, ctx)
    backs = share_cores(moves, backs, ctx)
    both = jnp.stack([asked, moves.send(after(asked, q), "core", 1)])
    far_asked = [moves.send(after(both, ctx), "y", kk) for kk in range(1, moves.yn)]
    rows_asked = jnp.stack([both] + far_asked).reshape(nd * slots)

    layer_out, gm, gml, dctx, gh, back_their, *back_mine = ff_call(
        me, n2, mid, cotangent, full_gain_two, ins, backs, square, tile
    )
    b_terms = core_sum(moves, back_their, back_mine)
    in_their, *in_mine = ff_in_call(me, after(n2, *far_asked), gh, rows)
    b_far = [summed([t[kk] for t in b_terms]).astype(BF16) for kk in range(1, moves.yn)]
    b_near = [moves.send(value, "y", kk + 1) for kk, value in enumerate(b_far)]
    i_terms = core_sum(moves, in_their, jnp.stack(in_mine))
    i_cut = [halves(moves, by_wide(moves, term), 0) for term in i_terms]
    i_keep = [c[0] for c in i_cut]
    i_send = after(summed([c[1] for c in i_cut]).astype(BF16), *b_far)
    i_got = send_wide(moves, i_send, 0)

    dq, dk, dv, dpre, sums = attn_back_call(after(dctx, i_send), probs, q, k, v, prefix, 4)

    b_cut = [
        halves(moves, by_wide(moves, term), 0)
        for term in [t[0] for t in b_terms] + [after(v, dq) for v in b_near]
    ]
    b_keep = [c[0] for c in b_cut]
    b_send = summed([c[1] for c in b_cut]).astype(BF16)
    b_got = send_wide(moves, b_send, 0)
    i_terms = i_keep + [after(i_got, b_send)]
    i_far = [summed([term[kk] for term in i_terms]).astype(BF16) for kk in range(1, moves.yn)]
    i_near = [moves.send(v, "y", kk + 1) for kk, v in enumerate(i_far)]

    returned = mm_tn(slot_hot, after(dpre, b_got, *i_near)).astype(BF16)
    arrived = lax.all_to_all(
        returned.reshape(nw, slots // nw, 4 * width), "wide", 0, 0, tiled=True
    )

    s_their, *s_mine = square_call(
        me, nd, rows, normed, after(ctx, *i_far), dq, dk, dv, gml, sums
    )
    s_terms = core_sum(moves, s_their, s_mine)

    def wide_step(value, bit, *deps):
        keep, send = halves(moves, value, bit)
        got = send_wide(moves, after(send.astype(BF16), *deps), bit)
        return keep + got.astype(F32), got

    p_sum = jnp.stack(
        [summed(b_keep + [after(b_got, s_their)]), summed([term[0] for term in i_terms] + i_near)]
    )
    s_far = [summed([t[kk] for t in s_terms]).astype(BF16) for kk in range(1, moves.yn)]
    s_near = [moves.send(value, "y", kk + 1) for kk, value in enumerate(s_far)]
    p_sum, p_first = wide_step(p_sum, 1, *s_far)

    for bit in range(2, moves.bits):
        p_sum, _ = wide_step(p_sum, bit, arrived)
    p_all = spread_wide(moves, p_sum[:, 0].astype(BF16).reshape(-1, width))
    p_all = p_all.reshape(nw, 2, -1, width)
    grad_back = p_all[:, 0].reshape(w_back.shape).astype(F32)
    grad_in = jnp.concatenate(
        cut(p_all[:, 1].reshape(-1, width), w_in.shape[1] // width, 0), axis=1
    ).astype(F32)

    grad_tokens = input_call(
        me, tokens, full_gain_one, after(gm, *s_far), dq, dk, dv, square, rows, tile
    )
    by_slot = arrived.reshape(slots, nd, 4 * width // nd)
    cols = by_distance([by_slot[:, j] for j in range(nd)], dp_index)
    got = moves.send(jnp.stack(cols[1::2]), "core", 1)
    pairs = [jnp.concatenate([cols[2 * kk], got[kk]], axis=0) for kk in range(moves.yn)]
    pairs_far = [
        moves.send(pairs[kk], "y", kk) for kk in range(1, moves.yn)
    ]
    table_rows = jnp.concatenate([pairs[0]] + pairs_far, axis=0)
    scatter = (jnp.arange(entries)[:, None] == rows_asked[None, :]).astype(BF16)
    grad_table = jnp.dot(scatter, table_rows, preferred_element_type=F32)

    s_sum = by_wide(moves, summed([t[0] for t in s_terms] + s_near))
    s_sum, _ = wide_step(s_sum, 0, grad_tokens, p_first)
    for bit in range(1, moves.bits):
        s_sum, _ = wide_step(s_sum, bit)
    grad_square = spread_wide(moves, s_sum[0].astype(BF16)).astype(F32)

    grad_query, grad_key, grad_value, grad_out = cut(grad_square[: 4 * rows], 4, 0)
    gain_grad = lambda gain, *pairs: sum(
        jnp.sum(weight.astype(F32) * grad, axis=1) for weight, grad in pairs
    ) / gain.astype(F32)
    return (
        layer_out,
        grad_tokens,
        grad_query,
        grad_key,
        grad_value,
        grad_out,
        grad_in,
        grad_back,
        gain_grad(gain_one, (w_query, grad_query), (w_key, grad_key), (w_value, grad_value)),
        gain_grad(gain_two, (w_in, grad_in)),
        grad_square[4 * rows : 4 * rows + NB // nd, :HEADS],
        grad_table,
    )


def solution(mesh):
    split = P(("dp", "wide"), None)
    weight = P("dp", None)
    return jax.shard_map(
        shards,
        mesh=mesh,
        in_specs=(split, P(("dp", "wide")), split, P("wide", None))
        + (weight,) * 6
        + (P("dp"), P("dp"), weight, split),
        out_specs=(split, split) + (weight,) * 6 + (P("dp"), P("dp"), weight, P("wide", "dp")),
        check_vma=False,
    )
```
